512 devices in a mesh: gx: 32 (over y_lo, z), gy: 16 (over x, y_hi, core).
Axes of the slice: x: 4, y: 8 (y_hi: 2, y_lo: 4; y = y_hi * 4 + y_lo), z: 8, core: 2. Of those that a mesh axis runs over, the one named last changes fastest.
Arguments:
- plume_field: float32 [32, 256, 256, 128], P(None, 'gx', 'gy'), may hold values from -6 to 6
- spectral_weight: bfloat16 [2, 2304, 48, 1024], P(None, 'gx', 'gy'), may hold values from -4 to 4, as said below
- point_weight: float32 [32, 32], replicated, may hold values from -1 to 1
- point_bias: float32 [32], replicated, may hold values from -3 to 3
Outputs:
- activated: float32 [32, 256, 256, 128], P(None, 'gx', 'gy')
The draws below stay inside these ranges and needn't reach their ends.
Inputs may be any that keep to these rules, and one draw needn't show every extreme that they name: `spectral_weight`: Real-valued entries.
All inputs are finite; a program needn't handle non-finite values.
Results may differ from the reference program's by a relative error of at most 0.0003.
Values sent between devices are 32-bit elements; how exact they have to be, the bound alone decides.
No kernel may reach another device: no remote copies, remote signals or barrier semaphores. Data moves between devices by JAX's collectives and lax.ppermute only.
A program may use at most 128 MiB of HBM per device.

```python
import jax
import jax.numpy as jnp
from jax import lax

C = 32
MX = 48
MY = 48
MZ = 48
NZ = 128
NX = 256
NY = 256


def draw_spectral_weight(key, part):
    key = jax.random.fold_in(key, 11)
    spread = (0.125 * NX * NY * NZ / (MX * MY * MZ * C)) ** 0.5
    shape = (2, MX * MY, MZ, C * C)
    values = jax.random.truncated_normal(key, -4.0, 4.0, shape, jnp.float32)
    return jnp.clip(values * spread, -4.0, 4.0).astype(jnp.bfloat16)


def block_scale(own_key, extent, split, least, high):
    def one(dim, parts):
        heights = jax.random.uniform(jax.random.fold_in(jax.random.fold_in(own_key, 6), dim), (parts,), jnp.float32, least / len(split), high / len(split))
        return jnp.repeat(jnp.exp(heights), extent[dim] // parts).reshape((-1,) + (1,) * (len(extent) - dim - 1))

    factor_of = one(*split[0])
    for cut in split[1:]:
        factor_of = factor_of * one(*cut)
    return factor_of


def gaussian(own_key, shape, scale, bound, cuts=(), kind=jnp.bfloat16):
    loudness = block_scale(own_key, shape, cuts, -0.22, 0.18) if cuts else 1.0
    entries = jax.random.normal(own_key, shape, jnp.float32) * scale * loudness
    return jnp.minimum(jnp.maximum(entries, -bound), bound).astype(kind)


def setup_inputs(seed: int = 0) -> dict:
    splits = jax.random.split(jax.random.key(seed), 5)
    return {
        "plume_field": gaussian(splits[0], (C, NX, NY, NZ), 1.0, 6.0, ((1, 32), (2, 16)), jnp.float32),
        "spectral_weight": draw_spectral_weight(jax.random.fold_in(splits[4], 71), 0),
        "point_weight": gaussian(splits[2], (C, C), C ** -0.5, 1.0, (), jnp.float32),
        "point_bias": gaussian(splits[3], (C,), 0.5, 3.0, (), jnp.float32),
    }


def kept_indices(kept, length):
    lower = jnp.arange(kept // 2, dtype=jnp.int32)
    return jnp.concatenate([lower, length - kept // 2 + lower]).astype(jnp.int32)


def reference(plume_field, spectral_weight, point_weight, point_bias):
    x_index = kept_indices(MX, NX)
    y_index = kept_indices(MY, NY)
    z_index = jnp.arange(MZ, dtype=jnp.int32)

    def forward(channel_field):
        spectrum = jnp.fft.rfft(channel_field, axis=2)[:, :, :MZ]
        spectrum = jnp.fft.fft(spectrum, axis=1)[:, y_index]
        return jnp.fft.fft(spectrum, axis=0)[x_index]

    spectra = lax.map(forward, plume_field)
    mixing = spectral_weight.reshape(2, MX, MY, MZ, C, C)

    def output_channel(index):
        column = jnp.moveaxis(mixing[..., index].astype(jnp.float32), 4, 1)
        mixed = jnp.sum(spectra * lax.complex(column[0], column[1]), axis=0)
        full_spectrum = jnp.zeros((NX, NY, NZ // 2 + 1), mixed.dtype)
        full_spectrum = full_spectrum.at[x_index[:, None, None], y_index[None, :, None], z_index[None, None, :]].set(mixed)
        spectral = jnp.fft.irfftn(full_spectrum, s=(NX, NY, NZ), axes=(0, 1, 2))
        linear = jnp.tensordot(point_weight[:, index], plume_field, axes=1, precision=lax.Precision.HIGHEST)
        return jax.nn.gelu(spectral + linear + point_bias[index], approximate=False)

    return lax.map(output_channel, jnp.arange(C, dtype=jnp.int32))
```

```python
import numpy as np

import jax
import jax.numpy as jnp
import ml_dtypes
from jax import lax
from jax.experimental import pallas as pl
from jax.experimental.pallas import tpu as pltpu
from jax.sharding import Mesh, PartitionSpec as P

F32 = jnp.float32
BF16 = jnp.bfloat16
GX = ("yl", "zz")
GY = ("px", "ph", "core")
C = 32
NX, NY, NZ = 256, 256, 128
M = 48
B = 64


def freq(i, kept=M):
    return np.where(i < kept // 2, i, i - kept)


def two(table):
    t = np.asarray(table, np.float32)
    hi = t.astype(ml_dtypes.bfloat16)
    lo = (t - hi.astype(np.float32)).astype(ml_dtypes.bfloat16)
    return hi, lo


def angle(f, pos, n):
    return 2.0 * np.pi * ((f * pos) % n) / n


def z_modes():
    d = np.arange(8)[:, None, None]
    h = np.arange(2)[None, :, None]
    k = np.arange(3)[None, None, :]
    return 3 * (4 * (d // 2) + 2 * h + d % 2) + k


def z_tables():
    g = z_modes().reshape(-1)
    th = angle(g[:, None], np.arange(NZ)[None, :], NZ)
    fwd = np.stack([np.cos(th), -np.sin(th)], axis=1).reshape(96, NZ)
    w = (np.where(g == 0, 1.0, 2.0) / (NX * NY * NZ))[:, None]
    inv = np.stack([np.cos(th) * w, -np.sin(th) * w], axis=1).reshape(96, NZ)
    return fwd, inv


def y_tables():
    f = freq(np.arange(M))
    d = np.arange(8)
    fwds, invs = [], []
    for h in range(2):
        pos = (64 * (d // 2) + 32 * h + 16 * (d % 2))[:, None] + np.arange(16)[None, :]
        th = angle(f[:, None], pos.reshape(1, -1), NY)
        cos, sin = np.zeros((B, 128)), np.zeros((B, 128))
        cos[:M], sin[:M] = np.cos(th), np.sin(th)
        fwds.append(np.block([[cos, sin], [-sin, cos]]))
        invs.append(np.block([[cos, sin], [-sin, cos]]).T)
    return np.stack(fwds), np.stack(invs)


def x_rows():
    gx = np.arange(32)
    first = 3 * (gx // 2) + gx % 2
    return np.stack([first, first + 1])


def x_tables():
    f = freq(x_rows().reshape(-1))
    th = angle(f[:, None], np.arange(NX)[None, :], NX)
    fwd = np.concatenate([np.cos(th), np.sin(th)])
    inv = np.concatenate([np.cos(th), np.sin(th)]).T
    return fwd, inv


def split(v):
    hi = v.astype(BF16)
    return hi, (v - hi.astype(F32)).astype(BF16)


def dot(a, b, dims=((1,), (0,))):
    return lax.dot_general(a, b, (dims, ((), ())), preferred_element_type=F32)


def dot3(a, b, dims=((1,), (0,))):
    return dot(a[0], b[0], dims) + dot(a[0], b[1], dims) + dot(a[1], b[0], dims)


NT = ((1,), (1,))


def z_kernel(field, t_hi, t_lo, out):
    t = (t_hi[...], t_lo[...])
    for y in range(16):
        a = split(field[pl.ds(y, 256, stride=16), :])
        r = dot3(t, a, NT)
        for half in range(2):
            out[pl.ds(half * 16 + y, 96, stride=32), :] = r[:, half * 128 : half * 128 + 128]


def y_kernel(rows, t_hi, t_lo, out):
    t = (t_hi[...], t_lo[...])
    for j in range(6):
        b = jnp.concatenate(
            [
                jnp.concatenate([rows[:, j, ri, half].reshape(128, 128) for ri in range(2)], axis=0)
                for half in range(2)
            ],
            axis=1,
        )
        r = dot3(t, split(b))
        h, k = j // 3, j % 3
        out[h * 32 : h * 32 + 32, k] = r.T.reshape(32, 8, 128)


def turn(v):
    rolled = pltpu.roll(v, B, 1)
    lane = lax.broadcasted_iota(jnp.int32, v.shape, 1)
    return jnp.where(lane < B, rolled, -rolled)


def x_kernel(rows, t_hi, t_lo, out):
    t = (t_hi[...], t_lo[...])
    zero = jnp.zeros((32, 128), F32)
    for k in range(3):
        s = (rows[0:32, k] + rows[32:64, k]).reshape(256, 128)
        r = dot3(t, split(s))
        m = r[:64] + turn(r[64:])
        for a in range(2):
            out[pl.ds(2 * k + a, 32, stride=8), :] = m[32 * a : 32 * a + 32]
    for a in range(6, 8):
        out[pl.ds(a, 32, stride=8), :] = zero


def mix_kernel(par, modes, w, expand, out, in_re, in_im, mid_re, mid_im):
    zero96 = jnp.zeros((96, 32), F32)
    start = pl.multiple_of(par[0] * 24, 8)
    e = expand[...]
    for k in range(3):
        for a in range(2):
            v = modes[pl.ds(2 * k + a, 32, stride=8), :].T
            in_re[k, a * 48 : a * 48 + 48, :] = v[:48]
            in_im[k, a * 48 : a * 48 + 48, :] = v[B : B + 48]
        mid_re[k] = zero96
        mid_im[k] = zero96
    for k in range(3):
        v = jnp.concatenate([in_re[k, pl.ds(start, 72), :], in_im[k, pl.ds(start, 72), :]], axis=0)
        hi, lo = split(v)
        wide = dot(hi, e) + dot(lo, e)
        re, im = wide[:72], wide[72:]
        w_re, w_im = w[0, k].astype(F32), w[1, k].astype(F32)
        for part, ref in ((re * w_re - im * w_im, mid_re), (re * w_im + im * w_re, mid_im)):
            s = part[:, 0:128]
            for i in range(1, 8):
                s = s + part[:, 128 * i : 128 * i + 128]
            s = s + pltpu.roll(s, 64, 1)
            s = s + pltpu.roll(s, 32, 1)
            ref[k, pl.ds(start, 72), :] = s[:, :32]
    pad = jnp.zeros((B - M, 32), F32)
    for k in range(3):
        for a in range(2):
            rows = slice(a * 48, a * 48 + 48)
            v = jnp.concatenate([mid_re[k, rows, :], pad, mid_im[k, rows, :], pad], axis=0)
            out[pl.ds(2 * k + a, 32, stride=8), :] = v.T
    for a in range(6, 8):
        out[pl.ds(a, 32, stride=8), :] = jnp.zeros((32, 128), F32)


def x_back_kernel(modes, t_hi, t_lo, out):
    t = (t_hi[...], t_lo[...])
    for k in range(3):
        v = jnp.concatenate([modes[pl.ds(2 * k + a, 32, stride=8), :] for a in range(2)], axis=0)
        r = dot3(t, split(jnp.concatenate([v, -turn(v)], axis=0))).reshape(32, 8, 128)
        out[0:32, k] = r
        out[32:64, k] = r


def y_back_kernel(rows, t_hi, t_lo, out):
    t = (t_hi[...], t_lo[...])
    for j in range(6):
        h, k = j // 3, j % 3
        v = rows[h * 32 : h * 32 + 32, k].reshape(256, 128)
        r = dot3(t, split(v), NT)
        for ri in range(2):
            for half in range(2):
                part = r[ri * 128 : ri * 128 + 128, half * 128 : half * 128 + 128]
                out[:, j, ri, half] = part.reshape(8, 16, 128)


def erf(x):
    return lax.erf(x)


def z_back_kernel(rows, field, t_hi, t_lo, mixing, bias, out):
    t = (t_hi[...], t_lo[...])
    kron = split(mixing[...])
    b = bias[...]
    for y in range(16):
        v = jnp.concatenate(
            [rows[pl.ds(half * 16 + y, 96, stride=32), :] for half in range(2)], axis=1
        ).T
        a = split(field[pl.ds(y, 256, stride=16), :])
        s = dot3(split(v), t) + dot3(kron, a) + b
        out[pl.ds(y, 256, stride=16), :] = 0.5 * s * (1.0 + erf(s * np.float32(np.sqrt(0.5))))


PARAMS = pltpu.CompilerParams(vmem_limit_bytes=40 * 1024 * 1024)


def call(kernel, shape, *operands, scratch=(), smem=0):
    specs = [
        pl.BlockSpec(memory_space=pltpu.SMEM if i < smem else pltpu.VMEM) for i in range(len(operands))
    ]
    return pl.pallas_call(
        kernel,
        out_shape=jax.ShapeDtypeStruct(shape, F32),
        in_specs=specs,
        out_specs=pl.BlockSpec(memory_space=pltpu.VMEM),
        scratch_shapes=list(scratch),
        compiler_params=PARAMS,
    )(*operands)


def exchange(v, axes):
    return lax.all_to_all(v, axes, 0, 0, tiled=True)


def on_device(field, weight, point_weight, point_bias):
    z_fwd, z_inv = z_tables()
    y_fwd, y_inv = y_tables()
    x_fwd, x_inv = x_tables()
    half = lax.axis_index("ph")
    pick = lambda table: [lax.dynamic_index_in_dim(jnp.asarray(t), half, 0, False) for t in two(table)]
    lines = field.reshape(C * 8 * 16, NZ)

    v = call(z_kernel, (3072, 128), lines, *two(z_fwd))
    v = exchange(v.reshape(8, 12, 2, 16, 128), ("px", "core"))
    v = call(y_kernel, (64, 3, 8, 128), v.reshape(8, 6, 2, 2, 16, 128), *pick(y_fwd))
    v = exchange(v, ("ph",) + GX)
    v = call(x_kernel, (256, 128), v, *two(x_fwd))
    v = exchange(v.reshape(32, 8, 128), GX)

    par = (lax.axis_index("zz") % 2).astype(jnp.int32).reshape(1)
    expand = np.kron(np.eye(C), np.ones((1, C))).astype(ml_dtypes.bfloat16)
    v = call(
        mix_kernel,
        (256, 128),
        par,
        v.reshape(256, 128),
        weight.transpose(0, 2, 1, 3),
        expand,
        scratch=[pltpu.VMEM((3, 96, 32), F32) for _ in range(4)],
        smem=1,
    )

    v = exchange(v.reshape(32, 8, 128), GX)
    v = call(x_back_kernel, (64, 3, 8, 128), v.reshape(256, 128), *two(x_inv))
    v = exchange(v, ("ph",) + GX)
    v = call(y_back_kernel, (8, 6, 2, 2, 16, 128), v, *pick(y_inv))
    v = exchange(v.reshape(8, 12, 2, 16, 128), ("px", "core"))
    kron = jnp.kron(point_weight.T, jnp.eye(8, dtype=F32))
    bias = jnp.broadcast_to(point_bias[:, None, None], (C, 8, 128)).reshape(256, 128)
    out = call(z_back_kernel, (4096, 128), v.reshape(3072, 128), lines, *two(z_inv), kron, bias)
    return out.reshape(C, 8, 16, NZ)


def solution(mesh):
    shape = (4, 8, 4, 2, 2)
    fine = Mesh(mesh.devices.reshape(shape), GX + GY)
    spec = P(None, GX, GY, None)
    return jax.shard_map(
        on_device,
        mesh=fine,
        in_specs=(spec, spec, P(), P()),
        out_specs=spec,
        check_vma=False,
    )
```

```python
import numpy as np

import jax
import jax.numpy as jnp
import ml_dtypes
from jax import lax
from jax.experimental import pallas as pl
from jax.experimental.pallas import tpu as pltpu
from jax.sharding import Mesh, PartitionSpec as P

F32 = jnp.float32
BF16 = jnp.bfloat16
GX = ("yl", "zz")
GY = ("px", "ph", "core")
C = 32
NX, NY, NZ = 256, 256, 128
M = 48
B = 64


def freq(i, kept=M):
    return np.where(i < kept // 2, i, i - kept)


def two(table):
    t = np.asarray(table, np.float32)
    hi = t.astype(ml_dtypes.bfloat16)
    lo = (t - hi.astype(np.float32)).astype(ml_dtypes.bfloat16)
    return np.stack([hi, lo])


def angle(f, pos, n):
    return 2.0 * np.pi * ((f * pos) % n) / n


def z_modes():
    d = np.arange(8)[:, None, None]
    h = np.arange(2)[None, :, None]
    k = np.arange(3)[None, None, :]
    return 3 * (4 * (d // 2) + 2 * h + d % 2) + k


def z_tables():
    g = z_modes().reshape(-1)
    th = angle(g[:, None], np.arange(NZ)[None, :], NZ)
    fwd = np.stack([np.cos(th), -np.sin(th)], axis=1).reshape(96, NZ)
    w = (np.where(g == 0, 1.0, 2.0) / (NX * NY * NZ))[:, None]
    inv = np.stack([np.cos(th) * w, -np.sin(th) * w], axis=1).reshape(96, NZ)
    return fwd, inv


def y_tables():
    f = freq(np.arange(M))
    d = np.arange(8)
    fwds, invs = [], []
    for h in range(2):
        pos = (64 * (d // 2) + 32 * h + 16 * (d % 2))[:, None] + np.arange(16)[None, :]
        th = angle(f[:, None], pos.reshape(1, -1), NY)
        cos, sin = np.zeros((B, 128)), np.zeros((B, 128))
        cos[:M], sin[:M] = np.cos(th), np.sin(th)
        fwds.append(np.block([[cos, sin], [-sin, cos]]))
        invs.append(np.block([[cos, sin], [-sin, cos]]).T)
    return np.stack(fwds), np.stack(invs)


def x_rows():
    gx = np.arange(32)
    first = 3 * (gx // 2) + gx % 2
    return np.stack([first, first + 1])


def x_tables():
    f = freq(x_rows().reshape(-1))
    pos = (8 * np.arange(32)[None, :] + np.arange(8)[:, None]).reshape(-1)
    th = angle(f[:, None], pos[None, :], NX)
    fwd = np.concatenate([np.cos(th), np.sin(th)])
    inv = np.concatenate([np.cos(th), np.sin(th)]).T
    return fwd, inv


def split(v):
    hi = v.astype(BF16)
    return hi, (v - hi.astype(F32)).astype(BF16)


def dot(a, b, dims=((1,), (0,))):
    return lax.dot_general(a, b, (dims, ((), ())), preferred_element_type=F32)


def dot3(a, b, dims=((1,), (0,))):
    return dot(a[0], b[0], dims) + dot(a[0], b[1], dims) + dot(a[1], b[0], dims)


NT = ((1,), (1,))


def lines_at(ref, y):
    return jnp.concatenate([ref[pl.ds(x * 16 + y, 32, stride=128), :] for x in range(8)], axis=0)


def z_kernel(field, table, out):
    t = (table[0], table[1])
    for y in range(16):
        r = dot3(t, split(lines_at(field, y)), NT)
        for half in range(2):
            out[pl.ds(half * 16 + y, 96, stride=32), :] = r[:, half * 128 : half * 128 + 128]


def y_kernel(rows, table, out):
    t = (table[0], table[1])
    for h in range(2):
        r = []
        for k in range(3):
            j = 3 * h + k
            b = jnp.concatenate(
                [
                    jnp.concatenate([rows[:, j, ri, half].reshape(128, 128) for ri in range(2)], axis=0)
                    for half in range(2)
                ],
                axis=1,
            )
            r.append(dot3(t, split(b)))
        for k in range(2):
            v = jnp.concatenate([r[k][:48], r[2][16 * k : 16 * k + 16], r[k][64:112], r[2][64 + 16 * k : 80 + 16 * k]], axis=0)
            v = v.T
            for x in range(8):
                out[pl.ds(h * 576 + k * 8 + x, 32, stride=18), :] = v[32 * x : 32 * x + 32]
        for xh in range(2):
            v = jnp.concatenate(
                [
                    r[2][64 * ri + 32 : 64 * ri + 48, 32 * x : 32 * x + 32]
                    for ri in range(2)
                    for x in range(4 * xh, 4 * xh + 4)
                ],
                axis=0,
            )
            out[pl.ds(h * 576 + 16 + xh, 32, stride=18), :] = v.T


def turn(v):
    rolled = pltpu.roll(v, B, 1)
    lane = lax.broadcasted_iota(jnp.int32, v.shape, 1)
    return jnp.where(lane < B, rolled, -rolled)


def x_kernel(rows, table, out):
    t = (table[0], table[1])
    at = lambda r: rows[pl.ds(r, 32, stride=18), :] + rows[pl.ds(576 + r, 32, stride=18), :]
    last = [at(16), at(17)]
    for k in range(3):
        if k < 2:
            s = [at(8 * k + x) for x in range(8)]
        else:
            s = [pltpu.roll(last[x // 4], (128 - 16 * (x % 4)) % 128, 1) for x in range(8)]
        r = dot3(t, split(jnp.concatenate(s, axis=0)))
        m = r[:64] + turn(r[64:])
        for a in range(2):
            out[pl.ds(2 * k + a, 32, stride=8), :] = m[32 * a : 32 * a + 32]
    for a in range(6, 8):
        out[pl.ds(a, 32, stride=8), :] = jnp.zeros((32, 128), F32)


def mix_kernel(par, modes, w, expand, out, in_re, in_im, mid_re, mid_im):
    start = pl.multiple_of(par[0] * 24, 8)
    e = expand[...]
    for a in range(2):
        v = [modes[pl.ds(2 * k + a, 32, stride=8), :].T for k in range(3)]
        for ref, o in ((in_re, 0), (in_im, B)):
            for k in range(2):
                ref[k, a * 48 : a * 48 + 48, :] = v[k][o : o + 48]
                ref[2, a * 48 + 16 * k : a * 48 + 16 * k + 16, :] = v[k][o + 48 : o + 64]
            ref[2, a * 48 + 32 : a * 48 + 48, :] = v[2][o : o + 16]
    for k in range(3):
        mid_re[k] = jnp.zeros((96, 32), F32)
        mid_im[k] = jnp.zeros((96, 32), F32)
    for k in range(3):
        v = jnp.concatenate([in_re[k, pl.ds(start, 72), :], in_im[k, pl.ds(start, 72), :]], axis=0)
        hi, lo = split(v)
        wide = dot(hi, e) + dot(lo, e)
        re, im = wide[:72], wide[72:]
        w_re, w_im = w[0, k].astype(F32), w[1, k].astype(F32)
        for part, ref in ((re * w_re - im * w_im, mid_re), (re * w_im + im * w_re, mid_im)):
            s = part[:, 0:128]
            for i in range(1, 8):
                s = s + part[:, 128 * i : 128 * i + 128]
            s = s + pltpu.roll(s, 64, 1)
            s = s + pltpu.roll(s, 32, 1)
            ref[k, pl.ds(start, 72), :] = s[:, :32]
    pad = jnp.zeros((B - 16, 32), F32)
    for a in range(2):
        for k in range(3):
            v = []
            for ref in (mid_re, mid_im):
                if k < 2:
                    v += [ref[k, a * 48 : a * 48 + 48, :], ref[2, a * 48 + 16 * k : a * 48 + 16 * k + 16, :]]
                else:
                    v += [ref[2, a * 48 + 32 : a * 48 + 48, :], pad]
            out[pl.ds(2 * k + a, 32, stride=8), :] = jnp.concatenate(v, axis=0).T
    for a in range(6, 8):
        out[pl.ds(a, 32, stride=8), :] = jnp.zeros((32, 128), F32)


def x_back_kernel(modes, table, out):
    t = (table[0], table[1])
    lane = lax.broadcasted_iota(jnp.int32, (32, 128), 1) % B
    for k in range(3):
        v = jnp.concatenate([modes[pl.ds(2 * k + a, 32, stride=8), :] for a in range(2)], axis=0)
        r = dot3(t, split(jnp.concatenate([v, -turn(v)], axis=0)))
        s = [r[32 * x : 32 * x + 32] for x in range(8)]
        if k == 2:
            packed = []
            for xh in range(2):
                v = s[4 * xh]
                for i in range(1, 4):
                    v = jnp.where(lane < 16 * i, v, pltpu.roll(s[4 * xh + i], 16 * i, 1))
                packed.append(v)
            s = packed
        for x in range(len(s)):
            for h in range(2):
                out[pl.ds(h * 576 + k * 8 + x, 32, stride=18), :] = s[x]


def y_back_kernel(rows, table, out):
    t = (table[0], table[1])
    lane = lax.broadcasted_iota(jnp.int32, (256, 128), 1) % B
    for h in range(2):
        at = lambda r: rows[pl.ds(h * 576 + r, 32, stride=18), :]
        v = [jnp.concatenate([at(8 * k + x) for x in range(8)], axis=0) for k in range(2)]
        last = [at(16), at(17)]
        v.append(
            jnp.concatenate([pltpu.roll(last[x // 4], (160 - 16 * (x % 4)) % 128, 1) for x in range(8)], axis=0)
        )
        v[2] = jnp.where(lane < 16, pltpu.roll(v[0], 80, 1), jnp.where(lane < 32, pltpu.roll(v[1], 96, 1), v[2]))
        for k in range(3):
            r = dot3(t, split(v[k]), NT)
            for ri in range(2):
                for half in range(2):
                    part = r[ri * 128 : ri * 128 + 128, half * 128 : half * 128 + 128]
                    out[:, 3 * h + k, ri, half] = part.reshape(8, 16, 128)


def point_kernel(field, weight, bias, out):
    w = jnp.concatenate([jnp.concatenate([weight[...]] * 8, axis=1)] * 8, axis=0)
    row = lax.broadcasted_iota(jnp.int32, (256, 256), 0) // 32
    col = lax.broadcasted_iota(jnp.int32, (256, 256), 1) // 32
    w = split(jnp.where(row == col, w, 0.0))
    b = jnp.concatenate([bias[...]] * 8, axis=0)
    for y in range(16):
        out[256 * y : 256 * y + 256, :] = dot3(w, split(lines_at(field, y))) + b


def z_back_kernel(rows, linear, table, out):
    t = (table[0], table[1])
    for y in range(16):
        v = jnp.concatenate(
            [rows[pl.ds(half * 16 + y, 96, stride=32), :] for half in range(2)], axis=1
        ).T
        s = dot3(split(v), t) + linear[256 * y : 256 * y + 256, :]
        s = 0.5 * s * (1.0 + lax.erf(s * np.float32(np.sqrt(0.5))))
        for x in range(8):
            out[pl.ds(x * 16 + y, 32, stride=128), :] = s[32 * x : 32 * x + 32]


PARAMS = pltpu.CompilerParams(vmem_limit_bytes=40 * 1024 * 1024)


def call(kernel, shape, *operands, scratch=(), smem=0, cost=None):
    specs = [
        pl.BlockSpec(memory_space=pltpu.SMEM if i < smem else pltpu.VMEM) for i in range(len(operands))
    ]
    return pl.pallas_call(
        kernel,
        out_shape=jax.ShapeDtypeStruct(shape, F32),
        in_specs=specs,
        out_specs=pl.BlockSpec(memory_space=pltpu.VMEM),
        scratch_shapes=list(scratch),
        compiler_params=PARAMS,
        cost_estimate=cost,
    )(*operands)


def exchange(v, axes):
    return lax.all_to_all(v, axes, 0, 0, tiled=True)


def on_device(field, weight, point_weight, point_bias):
    z_fwd, z_inv = z_tables()
    y_fwd, y_inv = y_tables()
    x_fwd, x_inv = x_tables()
    half = lax.axis_index("ph")
    pick = lambda table: lax.dynamic_index_in_dim(jnp.asarray(two(table)), half, 1, False)
    lines = field.reshape(C * 8 * 16, NZ)

    v = call(z_kernel, (3072, 128), lines, two(z_fwd))
    v = exchange(v.reshape(8, 12, 2, 16, 128), ("px", "core"))
    v = call(y_kernel, (1152, 128), v.reshape(8, 6, 2, 2, 16, 128), pick(y_fwd))
    v = exchange(v.reshape(64, 9, 2, 128), ("ph",) + GX)
    v = call(x_kernel, (256, 128), v.reshape(1152, 128), two(x_fwd))
    v = exchange(v.reshape(32, 8, 128), GX)

    par = (lax.axis_index("zz") % 2).astype(jnp.int32).reshape(1)
    expand = np.kron(np.eye(C), np.ones((1, C))).astype(ml_dtypes.bfloat16)
    v = call(
        mix_kernel,
        (256, 128),
        par,
        v.reshape(256, 128),
        weight.transpose(0, 2, 1, 3),
        expand,
        scratch=[pltpu.VMEM((3, 96, 32), F32) for _ in range(4)],
        smem=1,
    )

    v = exchange(v.reshape(32, 8, 128), GX)
    v = call(x_back_kernel, (1152, 128), v.reshape(256, 128), two(x_inv))
    v = exchange(v.reshape(64, 9, 2, 128), ("ph",) + GX)
    v = call(y_back_kernel, (8, 6, 2, 2, 16, 128), v.reshape(1152, 128), pick(y_inv))
    v = exchange(v.reshape(8, 12, 2, 16, 128), ("px", "core"))
    bias = jnp.broadcast_to(point_bias[:, None], (C, NZ))
    cost = pl.CostEstimate(flops=800_000_000, bytes_accessed=4 << 20, transcendentals=0)
    linear = call(point_kernel, (4096, 128), lines, point_weight.T, bias, cost=cost)
    out = call(z_back_kernel, (4096, 128), v.reshape(3072, 128), linear, two(z_inv))
    return out.reshape(C, 8, 16, NZ)


def solution(mesh):
    shape = (4, 8, 4, 2, 2)
    fine = Mesh(mesh.devices.reshape(shape), GX + GY)
    spec = P(None, GX, GY, None)
    return jax.shard_map(
        on_device,
        mesh=fine,
        in_specs=(spec, spec, P(), P()),
        out_specs=spec,
        check_vma=False,
    )
```

```python
import numpy as np

import jax
import jax.numpy as jnp
import ml_dtypes
from jax import lax
from jax.experimental import pallas as pl
from jax.experimental.pallas import tpu as pltpu
from jax.sharding import Mesh, PartitionSpec as P

F32 = jnp.float32
BF16 = jnp.bfloat16
GX = ("yl", "zz")
GY = ("px", "ph", "core")
C = 32
NX, NY, NZ = 256, 256, 128
M = 48
GX_OF = 8 * (np.arange(32) % 4) + np.arange(32) // 4
B = 64


def freq(i, kept=M):
    return np.where(i < kept // 2, i, i - kept)


def two(table):
    t = np.asarray(table, np.float32)
    hi = t.astype(ml_dtypes.bfloat16)
    lo = (t - hi.astype(np.float32)).astype(ml_dtypes.bfloat16)
    return np.stack([hi, lo])


def angle(f, pos, n):
    return 2.0 * np.pi * ((f * pos) % n) / n


def z_modes():
    d = np.arange(8)[:, None, None]
    h = np.arange(2)[None, :, None]
    k = np.arange(3)[None, None, :]
    return 3 * (4 * (d % 4) + 2 * h + d // 4) + k


def z_tables():
    g = z_modes().reshape(-1)
    th = angle(g[:, None], np.arange(NZ)[None, :], NZ)
    fwd = np.stack([np.cos(th), -np.sin(th)], axis=1).reshape(96, NZ)
    w = (np.where(g == 0, 1.0, 2.0) / (NX * NY * NZ))[:, None]
    inv = np.stack([np.cos(th) * w, -np.sin(th) * w], axis=1).reshape(96, NZ)
    return fwd, inv


def y_tables():
    f = freq(np.arange(M))
    d = np.arange(8)
    fwds, invs = [], []
    for h in range(2):
        pos = (64 * (d % 4) + 32 * h + 16 * (d // 4))[:, None] + np.arange(16)[None, :]
        th = angle(f[:, None], pos.reshape(1, -1), NY)
        cos, sin = np.zeros((B, 128)), np.zeros((B, 128))
        cos[:M], sin[:M] = np.cos(th), np.sin(th)
        fwds.append(np.block([[cos, sin], [-sin, cos]]))
        invs.append(np.block([[cos, sin], [-sin, cos]]).T)
    return np.stack(fwds), np.stack(invs)


def x_rows():
    gx = GX_OF
    first = 3 * (gx // 2) + gx % 2
    return np.stack([first, first + 1])


def x_tables():
    f = freq(x_rows().reshape(-1))
    pos = (8 * np.arange(32)[None, :] + np.arange(8)[:, None]).reshape(-1)
    th = angle(f[:, None], pos[None, :], NX)
    fwd = np.concatenate([np.cos(th), np.sin(th)])
    inv = np.concatenate([np.cos(th), np.sin(th)]).T
    return fwd, inv


def split(v):
    hi = v.astype(BF16)
    return hi, (v - hi.astype(F32)).astype(BF16)


def dot(a, b, dims=((1,), (0,))):
    return lax.dot_general(a, b, (dims, ((), ())), preferred_element_type=F32)


def dot3(a, b, dims=((1,), (0,))):
    return dot(a[0], b[0], dims) + dot(a[0], b[1], dims) + dot(a[1], b[0], dims)


NT = ((1,), (1,))


def lines_at(ref, y, ys=16):
    return jnp.concatenate([ref[pl.ds(x * ys + y, 32, stride=8 * ys), :] for x in range(8)], axis=0)


def z_kernel(field, table, out):
    t = (table[0], table[1])
    field = field.reshape(2048, 128)
    out = out.reshape(1536, 128)
    for y in range(8):
        r = dot3(t, split(lines_at(field, y, 8)), NT)
        for half in range(2):
            out[pl.ds(half * 8 + y, 96, stride=16), :] = r[:, half * 128 : half * 128 + 128]


def y_kernel(rows, table, out):
    t = (table[0], table[1])
    for h in range(2):
        r = []
        for k in range(3):
            j = 3 * h + k
            b = jnp.concatenate(
                [
                    jnp.concatenate([rows[:, j, ri, half].reshape(128, 128) for ri in range(2)], axis=0)
                    for half in range(2)
                ],
                axis=1,
            )
            r.append(dot3(t, split(b)))
        for k in range(2):
            v = jnp.concatenate([r[k][:48], r[2][16 * k : 16 * k + 16], r[k][64:112], r[2][64 + 16 * k : 80 + 16 * k]], axis=0)
            v = v.T
            for x in range(8):
                out[pl.ds(h * 18 + k * 8 + x, 32, stride=36), :] = v[32 * x : 32 * x + 32]
        for xh in range(2):
            v = jnp.concatenate(
                [
                    r[2][64 * ri + 32 : 64 * ri + 48, 32 * x : 32 * x + 32]
                    for ri in range(2)
                    for x in range(4 * xh, 4 * xh + 4)
                ],
                axis=0,
            )
            out[pl.ds(h * 18 + 16 + xh, 32, stride=36), :] = v.T


def turn(v):
    rolled = pltpu.roll(v, B, 1)
    lane = lax.broadcasted_iota(jnp.int32, v.shape, 1)
    return jnp.where(lane < B, rolled, -rolled)


def x_kernel(rows, table, out):
    t = (table[0], table[1])
    at = lambda r: rows[pl.ds(r, 32, stride=36), :] + rows[pl.ds(18 + r, 32, stride=36), :]
    last = [at(16), at(17)]
    for k in range(3):
        if k < 2:
            s = [at(8 * k + x) for x in range(8)]
        else:
            s = [pltpu.roll(last[x // 4], (128 - 16 * (x % 4)) % 128, 1) for x in range(8)]
        r = dot3(t, split(jnp.concatenate(s, axis=0)))
        m = r[:64] + turn(r[64:])
        for a in range(2):
            out[pl.ds(2 * k + a, 32, stride=8), :] = m[32 * a : 32 * a + 32]
    for a in range(6, 8):
        out[pl.ds(a, 32, stride=8), :] = jnp.zeros((32, 128), F32)


def mix_kernel(par, modes, w, expand, out, in_re, in_im, mid_re, mid_im):
    start = pl.multiple_of(par[0] * 24, 8)
    e = expand[...]
    for a in range(2):
        v = [modes[pl.ds(2 * k + a, 32, stride=8), :].T for k in range(3)]
        for ref, o in ((in_re, 0), (in_im, B)):
            for k in range(2):
                ref[k, a * 48 : a * 48 + 48, :] = v[k][o : o + 48]
                ref[2, a * 48 + 16 * k : a * 48 + 16 * k + 16, :] = v[k][o + 48 : o + 64]
            ref[2, a * 48 + 32 : a * 48 + 48, :] = v[2][o : o + 16]
    for k in range(3):
        mid_re[k] = jnp.zeros((96, 32), F32)
        mid_im[k] = jnp.zeros((96, 32), F32)
    for k in range(3):
        v = jnp.concatenate([in_re[k, pl.ds(start, 72), :], in_im[k, pl.ds(start, 72), :]], axis=0)
        hi, lo = split(v)
        wide = dot(hi, e) + dot(lo, e)
        re, im = wide[:72], wide[72:]
        w_re, w_im = w[0, k].astype(F32), w[1, k].astype(F32)
        for part, ref in ((re * w_re - im * w_im, mid_re), (re * w_im + im * w_re, mid_im)):
            s = part[:, 0:128]
            for i in range(1, 8):
                s = s + part[:, 128 * i : 128 * i + 128]
            s = s + pltpu.roll(s, 64, 1)
            s = s + pltpu.roll(s, 32, 1)
            ref[k, pl.ds(start, 72), :] = s[:, :32]
    pad = jnp.zeros((B - 16, 32), F32)
    for a in range(2):
        for k in range(3):
            v = []
            for ref in (mid_re, mid_im):
                if k < 2:
                    v += [ref[k, a * 48 : a * 48 + 48, :], ref[2, a * 48 + 16 * k : a * 48 + 16 * k + 16, :]]
                else:
                    v += [ref[2, a * 48 + 32 : a * 48 + 48, :], pad]
            v = jnp.concatenate(v, axis=0).T
            for yl in range(4):
                out[pl.ds(8 * yl + 2 * k + a, 8, stride=32), :] = v[8 * yl : 8 * yl + 8]
    for a in range(6, 8):
        out[pl.ds(a, 32, stride=8), :] = jnp.zeros((32, 128), F32)


def x_back_kernel(modes, table, out):
    t = (table[0], table[1])
    lane = lax.broadcasted_iota(jnp.int32, (32, 128), 1) % B
    for k in range(3):
        v = jnp.concatenate([modes[pl.ds(2 * k + a, 32, stride=8), :] for a in range(2)], axis=0)
        r = dot3(t, split(jnp.concatenate([v, -turn(v)], axis=0)))
        s = [r[32 * x : 32 * x + 32] for x in range(8)]
        if k == 2:
            packed = []
            for xh in range(2):
                v = s[4 * xh]
                for i in range(1, 4):
                    v = jnp.where(lane < 16 * i, v, pltpu.roll(s[4 * xh + i], 16 * i, 1))
                packed.append(v)
            s = packed
        for x in range(len(s)):
            for h in range(2):
                out[pl.ds(h * 18 + k * 8 + x, 32, stride=36), :] = s[x]


def y_back_kernel(rows, table, out):
    t = (table[0], table[1])
    lane = lax.broadcasted_iota(jnp.int32, (256, 128), 1) % B
    for h in range(2):
        at = lambda r: rows[pl.ds(h * 18 + r, 32, stride=36), :]
        v = [jnp.concatenate([at(8 * k + x) for x in range(8)], axis=0) for k in range(2)]
        last = [at(16), at(17)]
        v.append(
            jnp.concatenate([pltpu.roll(last[x // 4], (160 - 16 * (x % 4)) % 128, 1) for x in range(8)], axis=0)
        )
        v[2] = jnp.where(lane < 16, pltpu.roll(v[0], 80, 1), jnp.where(lane < 32, pltpu.roll(v[1], 96, 1), v[2]))
        for k in range(3):
            r = dot3(t, split(v[k]), NT)
            for ri in range(2):
                for half in range(2):
                    part = r[ri * 128 : ri * 128 + 128, half * 128 : half * 128 + 128]
                    out[:, 3 * h + k, ri, half] = part.reshape(8, 16, 128)


def point_kernel(field, weight, bias, out):
    w = jnp.concatenate([jnp.concatenate([weight[...]] * 8, axis=1)] * 8, axis=0)
    row = lax.broadcasted_iota(jnp.int32, (256, 256), 0) // 32
    col = lax.broadcasted_iota(jnp.int32, (256, 256), 1) // 32
    w = split(jnp.where(row == col, w, 0.0))
    b = jnp.concatenate([bias[...]] * 8, axis=0)
    for y in range(16):
        out[256 * y : 256 * y + 256, :] = dot3(w, split(lines_at(field, y))) + b


def z_back_kernel(rows, linear, table, out):
    t = (table[0], table[1])
    rows = rows.reshape(1536, 128)
    out = out.reshape(2048, 128)
    for y in range(8):
        v = jnp.concatenate(
            [rows[pl.ds(half * 8 + y, 96, stride=16), :] for half in range(2)], axis=1
        ).T
        s = dot3(split(v), t) + linear[256 * y : 256 * y + 256, :]
        s = 0.5 * s * (1.0 + lax.erf(s * np.float32(np.sqrt(0.5))))
        for x in range(8):
            out[pl.ds(x * 8 + y, 32, stride=64), :] = s[32 * x : 32 * x + 32]


PARAMS = pltpu.CompilerParams(vmem_limit_bytes=40 * 1024 * 1024)


def call(kernel, shape, *operands, scratch=(), smem=0, cost=None):
    specs = [
        pl.BlockSpec(memory_space=pltpu.SMEM if i < smem else pltpu.VMEM) for i in range(len(operands))
    ]
    return pl.pallas_call(
        kernel,
        out_shape=jax.ShapeDtypeStruct(shape, F32),
        in_specs=specs,
        out_specs=pl.BlockSpec(memory_space=pltpu.VMEM),
        scratch_shapes=list(scratch),
        compiler_params=PARAMS,
        cost_estimate=cost,
    )(*operands)


def halves(kernel, shape, *operands):
    def spec(dims):
        if len(dims) == 3 and dims[1] == 16:
            return pl.BlockSpec((dims[0], 8, dims[2]), lambda i: (0, i, 0))
        if dims == (4096, 128):
            return pl.BlockSpec((2048, 128), lambda i: (i, 0))
        return pl.BlockSpec(dims, lambda i: (0,) * len(dims))

    return pl.pallas_call(
        kernel,
        grid=(2,),
        out_shape=jax.ShapeDtypeStruct(shape, F32),
        in_specs=[spec(v.shape) for v in operands],
        out_specs=spec(shape),
        compiler_params=pltpu.CompilerParams(vmem_limit_bytes=60 * 1024 * 1024),
    )(*operands)


def exchange(v, axes):
    return lax.all_to_all(v, axes, 0, 0, tiled=True)


def on_device(field, weight, point_weight, point_bias):
    z_fwd, z_inv = z_tables()
    y_fwd, y_inv = y_tables()
    x_fwd, x_inv = x_tables()
    half = lax.axis_index("ph")
    pick = lambda table: lax.dynamic_index_in_dim(jnp.asarray(two(table)), half, 1, False)
    lines = field.reshape(C * 8 * 16, NZ)

    v = halves(z_kernel, (192, 16, 128), field.reshape(256, 16, 128), two(z_fwd))
    v = exchange(v.reshape(8, 12, 2, 16, 128), ("core", "px"))
    v = call(y_kernel, (1152, 128), v.reshape(8, 6, 2, 2, 16, 128), pick(y_fwd))
    v = exchange(v.reshape(64, 9, 2, 128), GX + ("ph",))
    v = call(x_kernel, (256, 128), v.reshape(1152, 128), two(x_fwd))
    v = exchange(v.reshape(32, 8, 128), ("zz", "yl"))

    par = (lax.axis_index("zz") % 2).astype(jnp.int32).reshape(1)
    expand = np.kron(np.eye(C)[GX_OF], np.ones((1, C))).astype(ml_dtypes.bfloat16)
    v = call(
        mix_kernel,
        (256, 128),
        par,
        v.reshape(256, 128),
        weight.transpose(0, 2, 1, 3),
        expand,
        scratch=[pltpu.VMEM((3, 96, 32), F32) for _ in range(4)],
        smem=1,
    )

    v = exchange(v.reshape(32, 8, 128), ("zz", "yl"))
    v = call(x_back_kernel, (1152, 128), v.reshape(256, 128), two(x_inv))
    v = exchange(v.reshape(64, 9, 2, 128), GX + ("ph",))
    v = call(y_back_kernel, (8, 6, 2, 2, 16, 128), v.reshape(1152, 128), pick(y_inv))
    v = exchange(v.reshape(8, 12, 2, 16, 128), ("core", "px"))
    bias = jnp.broadcast_to(point_bias[:, None], (C, NZ))
    cost = pl.CostEstimate(flops=800_000_000, bytes_accessed=4 << 20, transcendentals=0)
    linear = call(point_kernel, (4096, 128), lines, point_weight.T, bias, cost=cost)
    out = halves(z_back_kernel, (256, 16, 128), v.reshape(192, 16, 128), linear, two(z_inv))
    return out.reshape(C, 8, 16, NZ)


def solution(mesh):
    shape = (4, 8, 4, 2, 2)
    fine = Mesh(mesh.devices.reshape(shape), GX + GY)
    spec = P(None, GX, GY, None)
    return jax.shard_map(
        on_device,
        mesh=fine,
        in_specs=(spec, spec, P(), P()),
        out_specs=spec,
        check_vma=False,
    )
```

```python
import numpy as np

import jax
import jax.numpy as jnp
import ml_dtypes
from jax import lax
from jax.experimental import pallas as pl
from jax.experimental.pallas import tpu as pltpu
from jax.sharding import Mesh, PartitionSpec as P

F32 = jnp.float32
BF16 = jnp.bfloat16
GX = ("yl", "zz")
GY = ("px", "ph", "core")
C = 32
NX, NY, NZ = 256, 256, 128
M = 48
GX_OF = 8 * (np.arange(32) % 4) + np.arange(32) // 4
B = 64


def freq(i, kept=M):
    return np.where(i < kept // 2, i, i - kept)


def two(table):
    t = np.asarray(table, np.float32)
    hi = t.astype(ml_dtypes.bfloat16)
    lo = (t - hi.astype(np.float32)).astype(ml_dtypes.bfloat16)
    return np.stack([hi, lo])


def angle(f, pos, n):
    return 2.0 * np.pi * ((f * pos) % n) / n


def z_modes():
    d = np.arange(8)[:, None, None]
    h = np.arange(2)[None, :, None]
    k = np.arange(3)[None, None, :]
    return 3 * (4 * (d % 4) + 2 * h + d // 4) + k


def z_tables():
    g = z_modes().reshape(-1)
    th = angle(g[:, None], np.arange(NZ)[None, :], NZ)
    fwd = np.stack([np.cos(th), -np.sin(th)], axis=1).reshape(96, NZ)
    w = (np.where(g == 0, 1.0, 2.0) / (NX * NY * NZ))[:, None]
    inv = np.stack([np.cos(th) * w, -np.sin(th) * w], axis=1).reshape(96, NZ)
    return fwd, inv


def y_tables():
    f = freq(np.arange(M))
    d = np.arange(8)
    fwds, invs = [], []
    for h in range(2):
        pos = (64 * (d % 4) + 32 * h + 16 * (d // 4))[:, None] + np.arange(16)[None, :]
        th = angle(f[:, None], pos.reshape(1, -1), NY)
        cos, sin = np.zeros((B, 128)), np.zeros((B, 128))
        cos[:M], sin[:M] = np.cos(th), np.sin(th)
        fwds.append(np.block([[cos, sin], [-sin, cos]]))
        invs.append(np.block([[cos, sin], [-sin, cos]]).T)
    return np.stack(fwds), np.stack(invs)


def x_rows():
    gx = GX_OF
    first = 3 * (gx // 2) + gx % 2
    return np.stack([first, first + 1])


def x_tables():
    f = freq(x_rows().reshape(-1))
    pos = (8 * np.arange(32)[None, :] + np.arange(8)[:, None]).reshape(-1)
    th = angle(f[:, None], pos[None, :], NX)
    fwd = np.concatenate([np.cos(th), np.sin(th)])
    inv = np.concatenate([np.cos(th), np.sin(th)]).T
    return fwd, inv


def split(v):
    hi = v.astype(BF16)
    return hi, (v - hi.astype(F32)).astype(BF16)


def dot(a, b, dims=((1,), (0,))):
    return lax.dot_general(a, b, (dims, ((), ())), preferred_element_type=F32)


def dot3(a, b, dims=((1,), (0,))):
    return dot(a[0], b[0], dims) + dot(a[0], b[1], dims) + dot(a[1], b[0], dims)


NT = ((1,), (1,))


def lines_at(ref, y, xs=8, ys=16):
    return jnp.concatenate([ref[pl.ds(x * ys + y, 32, stride=xs * ys), :] for x in range(xs)], axis=0)


def z_kernel(field, table, out):
    t = table[...]
    field = field.reshape(1024, 128)
    out = out.reshape(768, 128)
    for y in range(8):
        a = jnp.concatenate(split(lines_at(field, y, 4, 8)), axis=1)
        r = dot(t, a, NT)
        out[pl.ds(y, 96, stride=8), :] = r[:96] + r[96:]


def y_kernel(rows, table, out):
    t = (table[0], table[1])
    for h in range(2):
        r = []
        for k in range(3):
            j = 3 * h + k
            b = jnp.concatenate(
                [
                    jnp.concatenate([rows[:, j, ri, half].reshape(128, 128) for ri in range(2)], axis=0)
                    for half in range(2)
                ],
                axis=1,
            )
            r.append(dot3(t, split(b)))
        for k in range(2):
            v = jnp.concatenate([r[k][:48], r[2][16 * k : 16 * k + 16], r[k][64:112], r[2][64 + 16 * k : 80 + 16 * k]], axis=0)
            v = v.T
            for x in range(8):
                out[pl.ds(h * 18 + k * 8 + x, 32, stride=36), :] = v[32 * x : 32 * x + 32]
        for xh in range(2):
            v = jnp.concatenate(
                [
                    r[2][64 * ri + 32 : 64 * ri + 48, 32 * x : 32 * x + 32]
                    for ri in range(2)
                    for x in range(4 * xh, 4 * xh + 4)
                ],
                axis=0,
            )
            out[pl.ds(h * 18 + 16 + xh, 32, stride=36), :] = v.T


def turn(v):
    rolled = pltpu.roll(v, B, 1)
    lane = lax.broadcasted_iota(jnp.int32, v.shape, 1)
    return jnp.where(lane < B, rolled, -rolled)


def x_kernel(rows, table, out):
    t = (table[0], table[1])
    at = lambda r: rows[pl.ds(r, 32, stride=36), :] + rows[pl.ds(18 + r, 32, stride=36), :]
    last = [at(16), at(17)]
    for k in range(3):
        if k < 2:
            s = [at(8 * k + x) for x in range(8)]
        else:
            s = [pltpu.roll(last[x // 4], (128 - 16 * (x % 4)) % 128, 1) for x in range(8)]
        r = dot3(t, split(jnp.concatenate(s, axis=0)))
        m = r[:64] + turn(r[64:])
        for a in range(2):
            out[pl.ds(2 * k + a, 32, stride=8), :] = m[32 * a : 32 * a + 32]
    for a in range(6, 8):
        out[pl.ds(a, 32, stride=8), :] = jnp.zeros((32, 128), F32)


def mix_kernel(par, modes, w, expand, out, in_re, in_im, mid_re, mid_im):
    start = pl.multiple_of(par[0] * 24, 8)
    e = expand[...]
    for a in range(2):
        v = [modes[pl.ds(2 * k + a, 32, stride=8), :].T for k in range(3)]
        for ref, o in ((in_re, 0), (in_im, B)):
            for k in range(2):
                ref[k, a * 48 : a * 48 + 48, :] = v[k][o : o + 48]
                ref[2, a * 48 + 16 * k : a * 48 + 16 * k + 16, :] = v[k][o + 48 : o + 64]
            ref[2, a * 48 + 32 : a * 48 + 48, :] = v[2][o : o + 16]
    for k in range(3):
        mid_re[k] = jnp.zeros((96, 32), F32)
        mid_im[k] = jnp.zeros((96, 32), F32)
    for k in range(3):
        v = jnp.concatenate([in_re[k, pl.ds(start, 72), :], in_im[k, pl.ds(start, 72), :]], axis=0)
        hi, lo = split(v)
        wide = dot(hi, e) + dot(lo, e)
        re, im = wide[:72], wide[72:]
        w_re, w_im = w[0, k].astype(F32), w[1, k].astype(F32)
        for part, ref in ((re * w_re - im * w_im, mid_re), (re * w_im + im * w_re, mid_im)):
            s = part[:, 0:128]
            for i in range(1, 8):
                s = s + part[:, 128 * i : 128 * i + 128]
            s = s + pltpu.roll(s, 64, 1)
            s = s + pltpu.roll(s, 32, 1)
            ref[k, pl.ds(start, 72), :] = s[:, :32]
    pad = jnp.zeros((B - 16, 32), F32)
    for a in range(2):
        for k in range(3):
            v = []
            for ref in (mid_re, mid_im):
                if k < 2:
                    v += [ref[k, a * 48 : a * 48 + 48, :], ref[2, a * 48 + 16 * k : a * 48 + 16 * k + 16, :]]
                else:
                    v += [ref[2, a * 48 + 32 : a * 48 + 48, :], pad]
            v = jnp.concatenate(v, axis=0).T
            for yl in range(4):
                out[pl.ds(8 * yl + 2 * k + a, 8, stride=32), :] = v[8 * yl : 8 * yl + 8]
    for a in range(6, 8):
        out[pl.ds(a, 32, stride=8), :] = jnp.zeros((32, 128), F32)


def x_back_kernel(modes, table, out):
    t = (table[0], table[1])
    lane = lax.broadcasted_iota(jnp.int32, (32, 128), 1) % B
    for k in range(3):
        v = jnp.concatenate([modes[pl.ds(2 * k + a, 32, stride=8), :] for a in range(2)], axis=0)
        r = dot3(t, split(jnp.concatenate([v, -turn(v)], axis=0)))
        s = [r[32 * x : 32 * x + 32] for x in range(8)]
        if k == 2:
            packed = []
            for xh in range(2):
                v = s[4 * xh]
                for i in range(1, 4):
                    v = jnp.where(lane < 16 * i, v, pltpu.roll(s[4 * xh + i], 16 * i, 1))
                packed.append(v)
            s = packed
        for x in range(len(s)):
            for h in range(2):
                out[pl.ds(h * 18 + k * 8 + x, 32, stride=36), :] = s[x]


def y_back_kernel(rows, table, out, work, sems):
    t = (table[0], table[1])
    lane = lax.broadcasted_iota(jnp.int32, (256, 128), 1) % B
    copies = []
    for h in range(2):
        at = lambda r: rows[pl.ds(h * 18 + r, 32, stride=36), :]
        v = [jnp.concatenate([at(8 * k + x) for x in range(8)], axis=0) for k in range(2)]
        last = [at(16), at(17)]
        v.append(
            jnp.concatenate([pltpu.roll(last[x // 4], (160 - 16 * (x % 4)) % 128, 1) for x in range(8)], axis=0)
        )
        v[2] = jnp.where(lane < 16, pltpu.roll(v[0], 80, 1), jnp.where(lane < 32, pltpu.roll(v[1], 96, 1), v[2]))
        for k in range(3):
            r = dot3(t, split(v[k]), NT)
            for ri in range(2):
                for half in range(2):
                    part = r[ri * 128 : ri * 128 + 128, half * 128 : half * 128 + 128]
                    work[3 * h + k, :, ri, half] = part.reshape(8, 16, 128)
            copies.append(pltpu.make_async_copy(work.at[3 * h + k], out.at[:, 3 * h + k], sems.at[3 * h + k]))
            copies[-1].start()
    for copy in copies:
        copy.wait()


def point_kernel(field, weight, bias, out):
    w = jnp.concatenate([jnp.concatenate([weight[...]] * 8, axis=1)] * 8, axis=0)
    row = lax.broadcasted_iota(jnp.int32, (256, 256), 0) // 32
    col = lax.broadcasted_iota(jnp.int32, (256, 256), 1) // 32
    w = split(jnp.where(row == col, w, 0.0))
    b = jnp.concatenate([bias[...]] * 8, axis=0)
    for y in range(16):
        out[y] = (dot3(w, split(lines_at(field, y))) + b).reshape(2, 128, 128)


def z_back_kernel(rows, linear, table, out):
    t = table[...]
    rows = rows.reshape(768, 128)
    linear = linear.reshape(1024, 128)
    out = out.reshape(1024, 128)
    for y in range(8):
        v = jnp.concatenate(split(rows[pl.ds(y, 96, stride=8), :]), axis=0)
        r = dot(v.T, t)
        s = r[:, :128] + r[:, 128:] + linear[128 * y : 128 * y + 128, :]
        s = 0.5 * s * (1.0 + lax.erf(s * np.float32(np.sqrt(0.5))))
        for x in range(4):
            out[pl.ds(x * 8 + y, 32, stride=32), :] = s[32 * x : 32 * x + 32]


PARAMS = pltpu.CompilerParams(vmem_limit_bytes=40 * 1024 * 1024)


def call(kernel, shape, *operands, scratch=(), smem=0, cost=None, place=pltpu.VMEM):
    specs = [
        pl.BlockSpec(memory_space=pltpu.SMEM if i < smem else pltpu.VMEM) for i in range(len(operands))
    ]
    return pl.pallas_call(
        kernel,
        out_shape=jax.ShapeDtypeStruct(shape, F32),
        in_specs=specs,
        out_specs=pl.BlockSpec(memory_space=place),
        scratch_shapes=list(scratch),
        compiler_params=PARAMS,
        cost_estimate=cost,
    )(*operands)


def quarters(kernel, shape, *operands):
    specs = {
        (32, 2, 4, 16, 128): pl.BlockSpec((32, 1, 4, 8, 128), lambda i, j: (0, j, 0, i, 0)),
        (96, 2, 16, 128): pl.BlockSpec((96, 1, 8, 128), lambda i, j: (0, j, i, 0)),
        (16, 2, 128, 128): pl.BlockSpec((8, 1, 128, 128), lambda i, j: (i, j, 0, 0)),
    }
    spec = lambda dims: specs.get(dims) or pl.BlockSpec(dims, lambda i, j: (0, 0))
    return pl.pallas_call(
        kernel,
        grid=(2, 2),
        out_shape=jax.ShapeDtypeStruct(shape, F32),
        in_specs=[spec(v.shape) for v in operands],
        out_specs=spec(shape),
        compiler_params=pltpu.CompilerParams(vmem_limit_bytes=60 * 1024 * 1024),
    )(*operands)


def exchange(v, axes):
    return lax.all_to_all(v, axes, 0, 0, tiled=True)


def on_device(field, weight, point_weight, point_bias):
    z_fwd, z_inv = z_tables()
    y_fwd, y_inv = y_tables()
    x_fwd, x_inv = x_tables()
    half = lax.axis_index("ph")
    pick = lambda table: lax.dynamic_index_in_dim(jnp.asarray(two(table)), half, 1, False)
    lines = field.reshape(C * 8 * 16, NZ)

    hi, lo = two(z_fwd)
    table = np.block([[hi, hi], [lo, np.zeros_like(lo)]])
    v = quarters(z_kernel, (96, 2, 16, 128), field.reshape(C, 2, 4, 16, NZ), table)
    v = exchange(v.reshape(8, 12, 2, 16, 128), ("core", "px"))
    v = call(y_kernel, (1152, 128), v.reshape(8, 6, 2, 2, 16, 128), pick(y_fwd))
    v = exchange(v.reshape(64, 9, 2, 128), GX + ("ph",))
    v = call(x_kernel, (256, 128), v.reshape(1152, 128), two(x_fwd))
    v = exchange(v.reshape(32, 8, 128), ("zz", "yl"))

    par = (lax.axis_index("zz") % 2).astype(jnp.int32).reshape(1)
    expand = np.kron(np.eye(C)[GX_OF], np.ones((1, C))).astype(ml_dtypes.bfloat16)
    v = call(
        mix_kernel,
        (256, 128),
        par,
        v.reshape(256, 128),
        weight.transpose(0, 2, 1, 3),
        expand,
        scratch=[pltpu.VMEM((3, 96, 32), F32) for _ in range(4)],
        smem=1,
    )

    v = exchange(v.reshape(32, 8, 128), ("zz", "yl"))
    v = call(x_back_kernel, (1152, 128), v.reshape(256, 128), two(x_inv))
    v = exchange(v.reshape(64, 9, 2, 128), GX + ("ph",))
    v = call(
        y_back_kernel,
        (8, 6, 2, 2, 16, 128),
        v.reshape(1152, 128),
        pick(y_inv),
        scratch=[pltpu.VMEM((6, 8, 2, 2, 16, 128), F32), pltpu.SemaphoreType.DMA((6,))],
        place=pltpu.HBM,
    )
    v = exchange(v.reshape(8, 12, 2, 16, 128), ("core", "px"))
    bias = jnp.broadcast_to(point_bias[:, None], (C, NZ))
    cost = pl.CostEstimate(flops=800_000_000, bytes_accessed=4 << 20, transcendentals=0)
    linear = call(point_kernel, (16, 2, 128, 128), lines, point_weight.T, bias, cost=cost)
    hi, lo = two(z_inv)
    table = np.block([[hi, lo], [hi, np.zeros_like(lo)]])
    out = quarters(z_back_kernel, (C, 2, 4, 16, NZ), v.reshape(96, 2, 16, 128), linear, table)
    return out.reshape(C, 8, 16, NZ)


def solution(mesh):
    shape = (4, 8, 4, 2, 2)
    fine = Mesh(mesh.devices.reshape(shape), GX + GY)
    spec = P(None, GX, GY, None)
    return jax.shard_map(
        on_device,
        mesh=fine,
        in_specs=(spec, spec, P(), P()),
        out_specs=spec,
        check_vma=False,
    )
```

```python
import numpy as np

import jax
import jax.numpy as jnp
import ml_dtypes
from jax import lax
from jax.experimental import pallas as pl
from jax.experimental.pallas import tpu as pltpu
from jax.sharding import Mesh, PartitionSpec as P

F32 = jnp.float32
BF16 = jnp.bfloat16
GX = ("yl", "zz")
GY = ("px", "ph", "core")
C = 32
NX, NY, NZ = 256, 256, 128
M = 48
GX_OF = 8 * (np.arange(32) % 4) + np.arange(32) // 4
B = 64


def freq(i, kept=M):
    return np.where(i < kept // 2, i, i - kept)


def two(table):
    t = np.asarray(table, np.float32)
    hi = t.astype(ml_dtypes.bfloat16)
    lo = (t - hi.astype(np.float32)).astype(ml_dtypes.bfloat16)
    return np.stack([hi, lo])


def angle(f, pos, n):
    return 2.0 * np.pi * ((f * pos) % n) / n


def z_modes():
    d = np.arange(8)[:, None, None]
    h = np.arange(2)[None, :, None]
    k = np.arange(3)[None, None, :]
    return 3 * (4 * (d % 4) + 2 * h + d // 4) + k


def z_tables():
    g = z_modes().reshape(-1)
    th = angle(g[:, None], np.arange(NZ)[None, :], NZ)
    fwd = np.stack([np.cos(th), -np.sin(th)], axis=1).reshape(96, NZ)
    w = (np.where(g == 0, 1.0, 2.0) / (NX * NY * NZ))[:, None]
    inv = np.stack([np.cos(th) * w, -np.sin(th) * w], axis=1).reshape(96, NZ)
    return fwd, inv


def y_tables():
    f = freq(np.arange(M))
    d = np.arange(8)
    fwds, invs = [], []
    for h in range(2):
        pos = (64 * (d % 4) + 32 * h + 16 * (d // 4))[:, None] + np.arange(16)[None, :]
        th = angle(f[:, None], pos.reshape(1, -1), NY)
        cos, sin = np.zeros((B, 128)), np.zeros((B, 128))
        cos[:M], sin[:M] = np.cos(th), np.sin(th)
        fwds.append(np.block([[cos, sin], [-sin, cos]]))
        invs.append(np.block([[cos, sin], [-sin, cos]]).T)
    return np.stack(fwds), np.stack(invs)


def x_rows():
    gx = GX_OF
    first = 3 * (gx // 2) + gx % 2
    return np.stack([first, first + 1])


def x_tables():
    f = freq(x_rows().reshape(-1))
    pos = (8 * np.arange(32)[None, :] + np.arange(8)[:, None]).reshape(-1)
    th = angle(f[:, None], pos[None, :], NX)
    fwd = np.concatenate([np.cos(th), np.sin(th)])
    inv = np.concatenate([np.cos(th), np.sin(th)]).T
    return fwd, inv


def split(v):
    hi = v.astype(BF16)
    return hi, (v - hi.astype(F32)).astype(BF16)


def dot(a, b, dims=((1,), (0,))):
    return lax.dot_general(a, b, (dims, ((), ())), preferred_element_type=F32)


def dot3(a, b, dims=((1,), (0,))):
    return dot(a[0], b[0], dims) + dot(a[0], b[1], dims) + dot(a[1], b[0], dims)


NT = ((1,), (1,))


def lines_at(ref, y):
    return jnp.concatenate([ref[pl.ds(x * 16 + y, 32, stride=128), :] for x in range(8)], axis=0)


CHUNKS = [(h, slice(4 * h, 4 * h + 4), slice(8 * i, 8 * i + 8)) for h in range(2) for i in range(2)]


def z_kernel(field, table, out, work, t, done, sems):
    copies = [pltpu.make_async_copy(table, t, sems.at[4])]
    for i, (h, xs, ys) in enumerate(CHUNKS):
        copies.append(pltpu.make_async_copy(field.at[:, xs, ys], work.at[:, xs, ys], sems.at[i]))
    for copy in copies:
        copy.start()
    copies[0].wait()
    for i, (h, xs, ys) in enumerate(CHUNKS):
        copies[i + 1].wait()
        by_y = [jnp.swapaxes(work[:, 4 * h + x, ys, :], 0, 1) for x in range(4)]
        modes = []
        for y in range(8):
            a = jnp.concatenate([v[y] for v in by_y], axis=0)
            r = dot(t[...], jnp.concatenate(split(a), axis=1), NT)
            modes.append(r[:96] + r[96:])
        done[:, h, ys, :] = jnp.swapaxes(jnp.stack(modes), 0, 1)
        copies.append(pltpu.make_async_copy(done.at[:, h, ys], out.at[:, h, ys], sems.at[5 + i]))
        copies[-1].start()
    for copy in copies[5:]:
        copy.wait()


def y_kernel(rows, table, out):
    half = lax.axis_index("ph")
    t = (table[0, half], table[1, half])
    for h in range(2):
        r = []
        for k in range(3):
            j = 3 * h + k
            b = jnp.concatenate(
                [
                    jnp.concatenate([rows[:, j, ri, half].reshape(128, 128) for ri in range(2)], axis=0)
                    for half in range(2)
                ],
                axis=1,
            )
            r.append(dot3(t, split(b)))
        for k in range(2):
            v = jnp.concatenate([r[k][:48], r[2][16 * k : 16 * k + 16], r[k][64:112], r[2][64 + 16 * k : 80 + 16 * k]], axis=0)
            v = v.T
            for x in range(8):
                out[pl.ds(h * 18 + k * 8 + x, 32, stride=36), :] = v[32 * x : 32 * x + 32]
        for xh in range(2):
            v = jnp.concatenate(
                [
                    r[2][64 * ri + 32 : 64 * ri + 48, 32 * x : 32 * x + 32]
                    for ri in range(2)
                    for x in range(4 * xh, 4 * xh + 4)
                ],
                axis=0,
            )
            out[pl.ds(h * 18 + 16 + xh, 32, stride=36), :] = v.T


def turn(v):
    rolled = pltpu.roll(v, B, 1)
    lane = lax.broadcasted_iota(jnp.int32, v.shape, 1)
    return jnp.where(lane < B, rolled, -rolled)


def x_kernel(rows, table, out):
    t = (table[0], table[1])
    at = lambda r: rows[pl.ds(r, 32, stride=36), :] + rows[pl.ds(18 + r, 32, stride=36), :]
    last = [at(16), at(17)]
    for k in range(3):
        if k < 2:
            s = [at(8 * k + x) for x in range(8)]
        else:
            s = [pltpu.roll(last[x // 4], (128 - 16 * (x % 4)) % 128, 1) for x in range(8)]
        r = dot3(t, split(jnp.concatenate(s, axis=0)))
        m = r[:64] + turn(r[64:])
        for a in range(2):
            out[pl.ds(2 * k + a, 32, stride=8), :] = m[32 * a : 32 * a + 32]
    for a in range(6, 8):
        out[pl.ds(a, 32, stride=8), :] = jnp.zeros((32, 128), F32)


def mix_kernel(modes, w, expand, out, in_re, in_im, mid_re, mid_im):
    start = pl.multiple_of(lax.axis_index("zz") % 2 * 24, 8)
    e = expand[...]
    for a in range(2):
        v = [modes[pl.ds(2 * k + a, 32, stride=8), :].T for k in range(3)]
        for ref, o in ((in_re, 0), (in_im, B)):
            for k in range(2):
                ref[k, a * 48 : a * 48 + 48, :] = v[k][o : o + 48]
                ref[2, a * 48 + 16 * k : a * 48 + 16 * k + 16, :] = v[k][o + 48 : o + 64]
            ref[2, a * 48 + 32 : a * 48 + 48, :] = v[2][o : o + 16]
    for k in range(3):
        mid_re[k] = jnp.zeros((96, 32), F32)
        mid_im[k] = jnp.zeros((96, 32), F32)
    for k in range(3):
        v = jnp.concatenate([in_re[k, pl.ds(start, 72), :], in_im[k, pl.ds(start, 72), :]], axis=0)
        hi, lo = split(v)
        wide = dot(hi, e) + dot(lo, e)
        re, im = wide[:72], wide[72:]
        w_re, w_im = w[0, k].astype(F32), w[1, k].astype(F32)
        for part, ref in ((re * w_re - im * w_im, mid_re), (re * w_im + im * w_re, mid_im)):
            s = part[:, 0:128]
            for i in range(1, 8):
                s = s + part[:, 128 * i : 128 * i + 128]
            s = s + pltpu.roll(s, 64, 1)
            s = s + pltpu.roll(s, 32, 1)
            ref[k, pl.ds(start, 72), :] = s[:, :32]
    pad = jnp.zeros((B - 16, 32), F32)
    for a in range(2):
        for k in range(3):
            v = []
            for ref in (mid_re, mid_im):
                if k < 2:
                    v += [ref[k, a * 48 : a * 48 + 48, :], ref[2, a * 48 + 16 * k : a * 48 + 16 * k + 16, :]]
                else:
                    v += [ref[2, a * 48 + 32 : a * 48 + 48, :], pad]
            v = jnp.concatenate(v, axis=0).T
            for yl in range(4):
                out[pl.ds(8 * yl + 2 * k + a, 8, stride=32), :] = v[8 * yl : 8 * yl + 8]
    for a in range(6, 8):
        out[pl.ds(a, 32, stride=8), :] = jnp.zeros((32, 128), F32)


def x_back_kernel(modes, table, out):
    t = (table[0], table[1])
    lane = lax.broadcasted_iota(jnp.int32, (32, 128), 1) % B
    for k in range(3):
        v = jnp.concatenate([modes[pl.ds(2 * k + a, 32, stride=8), :] for a in range(2)], axis=0)
        r = dot3(t, split(jnp.concatenate([v, -turn(v)], axis=0)))
        s = [r[32 * x : 32 * x + 32] for x in range(8)]
        if k == 2:
            packed = []
            for xh in range(2):
                v = s[4 * xh]
                for i in range(1, 4):
                    v = jnp.where(lane < 16 * i, v, pltpu.roll(s[4 * xh + i], 16 * i, 1))
                packed.append(v)
            s = packed
        for x in range(len(s)):
            for h in range(2):
                out[pl.ds(h * 18 + k * 8 + x, 32, stride=36), :] = s[x]


def y_back_kernel(rows, table, out):
    half = lax.axis_index("ph")
    t = (table[0, half], table[1, half])
    lane = lax.broadcasted_iota(jnp.int32, (256, 128), 1) % B
    for h in range(2):
        at = lambda r: rows[pl.ds(h * 18 + r, 32, stride=36), :]
        v = [jnp.concatenate([at(8 * k + x) for x in range(8)], axis=0) for k in range(2)]
        last = [at(16), at(17)]
        v.append(
            jnp.concatenate([pltpu.roll(last[x // 4], (160 - 16 * (x % 4)) % 128, 1) for x in range(8)], axis=0)
        )
        v[2] = jnp.where(lane < 16, pltpu.roll(v[0], 80, 1), jnp.where(lane < 32, pltpu.roll(v[1], 96, 1), v[2]))
        for k in range(3):
            r = dot3(t, split(v[k]), NT)
            for ri in range(2):
                for half in range(2):
                    part = r[ri * 128 : ri * 128 + 128, half * 128 : half * 128 + 128]
                    out[:, 3 * h + k, ri, half] = part.reshape(8, 16, 128)


def point_kernel(field, weight, bias, out):
    w = jnp.concatenate([jnp.concatenate([weight[...]] * 8, axis=1)] * 8, axis=0)
    row = lax.broadcasted_iota(jnp.int32, (256, 256), 0) // 32
    col = lax.broadcasted_iota(jnp.int32, (256, 256), 1) // 32
    w = split(jnp.where(row == col, w, 0.0))
    b = jnp.concatenate([bias[...]] * 8, axis=0)
    for y in range(16):
        out[y] = (dot3(w, split(lines_at(field, y))) + b).reshape(2, 128, 128)


def z_back_kernel(rows, linear, table, out, work, sems):
    t = table[...]
    copies = []
    for i, (h, xs, ys) in enumerate(CHUNKS):
        by_y = jnp.swapaxes(rows[:, h, ys, :], 0, 1)
        cells = []
        for y in range(8):
            r = dot(jnp.concatenate(split(by_y[y]), axis=0).T, t)
            s = r[:, :128] + r[:, 128:] + linear[ys.start + y, h]
            cells.append(0.5 * s * (1.0 + lax.erf(s * np.float32(np.sqrt(0.5)))))
        cells = jnp.stack(cells)
        for x in range(4):
            work[:, 4 * h + x, ys, :] = jnp.swapaxes(cells[:, 32 * x : 32 * x + 32], 0, 1)
        copies.append(pltpu.make_async_copy(work.at[:, xs, ys], out.at[:, xs, ys], sems.at[i]))
        copies[-1].start()
    for copy in copies:
        copy.wait()


VMEM = pl.BlockSpec(memory_space=pltpu.VMEM)
ANY = pl.BlockSpec(memory_space=pl.ANY)


def call(kernel, shape, *operands, ins=VMEM, outs=VMEM, scratch=(), limit=24, cost=None):
    return pl.pallas_call(
        kernel,
        out_shape=jax.ShapeDtypeStruct(shape, F32),
        in_specs=[ins] * len(operands),
        out_specs=outs,
        scratch_shapes=list(scratch),
        compiler_params=pltpu.CompilerParams(vmem_limit_bytes=limit * 1024 * 1024),
        cost_estimate=cost,
    )(*operands)


def exchange(v, axes):
    return lax.all_to_all(v, axes, 0, 0, tiled=True)


def on_device(field, weight, point_weight, point_bias):
    z_fwd, z_inv = z_tables()
    y_fwd, y_inv = y_tables()
    x_fwd, x_inv = x_tables()
    block = pltpu.VMEM((C, 8, 16, NZ), F32)

    hi, lo = two(z_fwd)
    table = np.block([[hi, hi], [lo, np.zeros_like(lo)]])
    scratch = [block, pltpu.VMEM(table.shape, BF16), pltpu.VMEM((96, 2, 16, 128), F32), pltpu.SemaphoreType.DMA((9,))]
    v = call(z_kernel, (96, 2, 16, 128), field, table, ins=ANY, outs=ANY, scratch=scratch, limit=60)
    v = exchange(v.reshape(8, 12, 2, 16, 128), ("core", "px"))
    v = call(y_kernel, (1152, 128), v.reshape(8, 6, 2, 2, 16, 128), two(y_fwd))
    v = exchange(v.reshape(64, 9, 2, 128), GX + ("ph",))
    v = call(x_kernel, (256, 128), v.reshape(1152, 128), two(x_fwd))

    v, again = lax.optimization_barrier((v, field))
    bias = jnp.broadcast_to(point_bias[:, None], (C, NZ))
    cost = pl.CostEstimate(flops=800_000_000, bytes_accessed=4 << 20, transcendentals=0)
    linear = call(point_kernel, (16, 2, 128, 128), again.reshape(C * 8 * 16, NZ), point_weight.T, bias, cost=cost)
    v = exchange(v.reshape(32, 8, 128), ("zz", "yl"))
    v, linear = lax.optimization_barrier((v, linear))

    expand = np.kron(np.eye(C)[GX_OF], np.ones((1, C))).astype(ml_dtypes.bfloat16)
    scratch = [pltpu.VMEM((3, 96, 32), F32) for _ in range(4)]
    v = call(mix_kernel, (256, 128), v.reshape(256, 128), weight.transpose(0, 2, 1, 3), expand, scratch=scratch)

    v = exchange(v.reshape(32, 8, 128), ("zz", "yl"))
    v = call(x_back_kernel, (1152, 128), v.reshape(256, 128), two(x_inv))
    v = exchange(v.reshape(64, 9, 2, 128), GX + ("ph",))
    v = call(y_back_kernel, (8, 6, 2, 2, 16, 128), v.reshape(1152, 128), two(y_inv))
    v = exchange(v.reshape(8, 12, 2, 16, 128), ("core", "px"))
    hi, lo = two(z_inv)
    table = np.block([[hi, lo], [hi, np.zeros_like(lo)]])
    scratch = [block, pltpu.SemaphoreType.DMA((4,))]
    return call(
        z_back_kernel, (C, 8, 16, NZ), v.reshape(96, 2, 16, 128), linear, table, outs=ANY, scratch=scratch
    )


def solution(mesh):
    shape = (4, 8, 4, 2, 2)
    fine = Mesh(mesh.devices.reshape(shape), GX + GY)
    spec = P(None, GX, GY, None)
    return jax.shard_map(
        on_device,
        mesh=fine,
        in_specs=(spec, spec, P(), P()),
        out_specs=spec,
        check_vma=False,
    )
```

```python
import numpy as np

import jax
import jax.numpy as jnp
import ml_dtypes
from jax import lax
from jax.experimental import pallas as pl
from jax.experimental.pallas import tpu as pltpu
from jax.sharding import Mesh, PartitionSpec as P

F32 = jnp.float32
BF16 = jnp.bfloat16
GX = ("yl", "zz")
GY = ("px", "ph", "core")
C = 32
NX, NY, NZ = 256, 256, 128
M = 48
GX_OF = 8 * (np.arange(32) % 4) + np.arange(32) // 4
B = 64


def freq(i, kept=M):
    return np.where(i < kept // 2, i, i - kept)


def two(table):
    t = np.asarray(table, np.float32)
    hi = t.astype(ml_dtypes.bfloat16)
    lo = (t - hi.astype(np.float32)).astype(ml_dtypes.bfloat16)
    return np.stack([hi, lo])


def angle(f, pos, n):
    return 2.0 * np.pi * ((f * pos) % n) / n


def z_modes():
    d = np.arange(8)[:, None, None]
    h = np.arange(2)[None, :, None]
    k = np.arange(3)[None, None, :]
    return 3 * (4 * (d % 4) + 2 * h + d // 4) + k


def z_inverse():
    g = z_modes().reshape(-1)
    th = angle(g[:, None], np.arange(NZ)[None, :], NZ)
    w = (np.where(g == 0, 1.0, 2.0) / (NX * NY * NZ))[:, None]
    return np.stack([np.cos(th) * w, -np.sin(th) * w], axis=1).reshape(96, NZ)


def y_tables():
    f = freq(np.arange(M))
    d = np.arange(8)
    fwds, invs = [], []
    for h in range(2):
        pos = (64 * (d % 4) + 32 * h + 16 * (d // 4))[:, None] + np.arange(16)[None, :]
        th = angle(f[:, None], pos.reshape(1, -1), NY)
        cos, sin = np.zeros((B, 128)), np.zeros((B, 128))
        cos[:M], sin[:M] = np.cos(th), np.sin(th)
        fwds.append(np.block([[cos, sin], [-sin, cos]]))
        invs.append(np.block([[cos, sin], [-sin, cos]]).T)
    return np.stack(fwds), np.stack(invs)


def x_rows():
    gx = GX_OF
    first = 3 * (gx // 2) + gx % 2
    return np.stack([first, first + 1])


def x_tables():
    f = freq(x_rows().reshape(-1))
    pos = (8 * np.arange(32)[None, :] + np.arange(8)[:, None]).reshape(-1)
    th = angle(f[:, None], pos[None, :], NX)
    fwd = np.concatenate([np.cos(th), np.sin(th)])
    inv = np.concatenate([np.cos(th), np.sin(th)]).T
    return fwd, inv


def split(v):
    hi = v.astype(BF16)
    return hi, (v - hi.astype(F32)).astype(BF16)


def dot(a, b, dims=((1,), (0,))):
    return lax.dot_general(a, b, (dims, ((), ())), preferred_element_type=F32)


def dot3(a, b, dims=((1,), (0,))):
    return dot(a[0], b[0], dims) + dot(a[0], b[1], dims) + dot(a[1], b[0], dims)


NT = ((1,), (1,))


def lines_at(ref, y):
    return jnp.concatenate([ref[pl.ds(x * 16 + y, 32, stride=128), :] for x in range(8)], axis=0)


CHUNKS = [(h, slice(4 * h, 4 * h + 4), slice(8 * i, 8 * i + 8)) for h in range(2) for i in range(2)]


def z_table():
    m = lax.broadcasted_iota(jnp.int32, (96, NZ), 0).astype(F32)
    z = lax.broadcasted_iota(jnp.int32, (96, NZ), 1).astype(F32)
    d = jnp.floor((m + 0.5) * np.float32(1 / 12))
    j = jnp.floor((m - 12 * d + 0.5) * np.float32(1 / 2))
    ri = m - 12 * d - 2 * j
    q = jnp.floor(d * np.float32(1 / 4))
    h = jnp.floor((j + 0.5) * np.float32(1 / 3))
    g = 3 * (4 * (d - 4 * q) + 2 * h + q) + (j - 3 * h)
    turns = g * z + 32 * ri
    turns = turns - 128 * jnp.floor(turns * np.float32(1 / 128) + 0.5)
    return jnp.cos(turns * np.float32(2 * np.pi / 128))


def z_kernel(field, out, work, sems):
    copies = []
    for h in range(2):
        xs = slice(4 * h, 4 * h + 4)
        copies.append(pltpu.make_async_copy(field.at[:, xs], work.at[:, xs], sems.at[h]))
        copies[h].start()
    hi, lo = split(z_table())
    t = jnp.concatenate(
        [jnp.concatenate([hi, hi], axis=1), jnp.concatenate([lo, jnp.zeros_like(lo)], axis=1)], axis=0
    )
    for h, xs, ys in CHUNKS:
        if ys.start == 0:
            copies[h].wait()
        by_y = [jnp.swapaxes(work[:, 4 * h + x, ys, :], 0, 1) for x in range(4)]
        modes = []
        for y in range(8):
            a = jnp.concatenate([v[y] for v in by_y], axis=0)
            r = dot(t, jnp.concatenate(split(a), axis=1), NT)
            modes.append(r[:96] + r[96:])
        out[:, h, ys, :] = jnp.swapaxes(jnp.stack(modes), 0, 1)


def y_kernel(rows, table, out):
    half = lax.axis_index("ph")
    t = (table[0, half], table[1, half])
    for h in range(2):
        r = []
        for k in range(3):
            j = 3 * h + k
            b = jnp.concatenate(
                [
                    jnp.concatenate([rows[:, j, ri, half].reshape(128, 128) for ri in range(2)], axis=0)
                    for half in range(2)
                ],
                axis=1,
            )
            r.append(dot3(t, split(b)))
        for k in range(2):
            v = jnp.concatenate([r[k][:48], r[2][16 * k : 16 * k + 16], r[k][64:112], r[2][64 + 16 * k : 80 + 16 * k]], axis=0)
            v = v.T
            for x in range(8):
                out[pl.ds(h * 18 + k * 8 + x, 32, stride=36), :] = v[32 * x : 32 * x + 32]
        for xh in range(2):
            v = jnp.concatenate(
                [
                    r[2][64 * ri + 32 : 64 * ri + 48, 32 * x : 32 * x + 32]
                    for ri in range(2)
                    for x in range(4 * xh, 4 * xh + 4)
                ],
                axis=0,
            )
            out[pl.ds(h * 18 + 16 + xh, 32, stride=36), :] = v.T


def turn(v):
    rolled = pltpu.roll(v, B, 1)
    lane = lax.broadcasted_iota(jnp.int32, v.shape, 1)
    return jnp.where(lane < B, rolled, -rolled)


def x_kernel(rows, table, out):
    t = (table[0], table[1])
    at = lambda r: rows[pl.ds(r, 32, stride=36), :] + rows[pl.ds(18 + r, 32, stride=36), :]
    last = [at(16), at(17)]
    for k in range(3):
        if k < 2:
            s = [at(8 * k + x) for x in range(8)]
        else:
            s = [pltpu.roll(last[x // 4], (128 - 16 * (x % 4)) % 128, 1) for x in range(8)]
        r = dot3(t, split(jnp.concatenate(s, axis=0)))
        m = r[:64] + turn(r[64:])
        for a in range(2):
            out[pl.ds(2 * k + a, 32, stride=8), :] = m[32 * a : 32 * a + 32]
    for a in range(6, 8):
        out[pl.ds(a, 32, stride=8), :] = jnp.zeros((32, 128), F32)


def mix_kernel(modes, w, expand, out, in_re, in_im, mid_re, mid_im):
    start = pl.multiple_of(lax.axis_index("zz") % 2 * 24, 8)
    e = expand[...]
    for a in range(2):
        v = [modes[pl.ds(2 * k + a, 32, stride=8), :].T for k in range(3)]
        for ref, o in ((in_re, 0), (in_im, B)):
            for k in range(2):
                ref[k, a * 48 : a * 48 + 48, :] = v[k][o : o + 48]
                ref[2, a * 48 + 16 * k : a * 48 + 16 * k + 16, :] = v[k][o + 48 : o + 64]
            ref[2, a * 48 + 32 : a * 48 + 48, :] = v[2][o : o + 16]
    for k in range(3):
        mid_re[k] = jnp.zeros((96, 32), F32)
        mid_im[k] = jnp.zeros((96, 32), F32)
    for k in range(3):
        v = jnp.concatenate([in_re[k, pl.ds(start, 72), :], in_im[k, pl.ds(start, 72), :]], axis=0)
        hi, lo = split(v)
        wide = dot(hi, e) + dot(lo, e)
        re, im = wide[:72], wide[72:]
        w_re, w_im = w[0, k].astype(F32), w[1, k].astype(F32)
        for part, ref in ((re * w_re - im * w_im, mid_re), (re * w_im + im * w_re, mid_im)):
            s = part[:, 0:128]
            for i in range(1, 8):
                s = s + part[:, 128 * i : 128 * i + 128]
            s = s + pltpu.roll(s, 64, 1)
            s = s + pltpu.roll(s, 32, 1)
            ref[k, pl.ds(start, 72), :] = s[:, :32]
    pad = jnp.zeros((B - 16, 32), F32)
    for a in range(2):
        for k in range(3):
            v = []
            for ref in (mid_re, mid_im):
                if k < 2:
                    v += [ref[k, a * 48 : a * 48 + 48, :], ref[2, a * 48 + 16 * k : a * 48 + 16 * k + 16, :]]
                else:
                    v += [ref[2, a * 48 + 32 : a * 48 + 48, :], pad]
            v = jnp.concatenate(v, axis=0).T
            for yl in range(4):
                out[pl.ds(8 * yl + 2 * k + a, 8, stride=32), :] = v[8 * yl : 8 * yl + 8]
    for a in range(6, 8):
        out[pl.ds(a, 32, stride=8), :] = jnp.zeros((32, 128), F32)


def x_back_kernel(modes, table, out):
    t = (table[0], table[1])
    lane = lax.broadcasted_iota(jnp.int32, (32, 128), 1) % B
    for k in range(3):
        v = jnp.concatenate([modes[pl.ds(2 * k + a, 32, stride=8), :] for a in range(2)], axis=0)
        r = dot3(t, split(jnp.concatenate([v, -turn(v)], axis=0)))
        s = [r[32 * x : 32 * x + 32] for x in range(8)]
        if k == 2:
            packed = []
            for xh in range(2):
                v = s[4 * xh]
                for i in range(1, 4):
                    v = jnp.where(lane < 16 * i, v, pltpu.roll(s[4 * xh + i], 16 * i, 1))
                packed.append(v)
            s = packed
        for x in range(len(s)):
            for h in range(2):
                out[pl.ds(h * 18 + k * 8 + x, 32, stride=36), :] = s[x]


def y_back_kernel(rows, table, out):
    half = lax.axis_index("ph")
    t = (table[0, half], table[1, half])
    lane = lax.broadcasted_iota(jnp.int32, (256, 128), 1) % B
    for h in range(2):
        at = lambda r: rows[pl.ds(h * 18 + r, 32, stride=36), :]
        v = [jnp.concatenate([at(8 * k + x) for x in range(8)], axis=0) for k in range(2)]
        last = [at(16), at(17)]
        v.append(
            jnp.concatenate([pltpu.roll(last[x // 4], (160 - 16 * (x % 4)) % 128, 1) for x in range(8)], axis=0)
        )
        v[2] = jnp.where(lane < 16, pltpu.roll(v[0], 80, 1), jnp.where(lane < 32, pltpu.roll(v[1], 96, 1), v[2]))
        for k in range(3):
            r = dot3(t, split(v[k]), NT)
            for ri in range(2):
                for half in range(2):
                    part = r[ri * 128 : ri * 128 + 128, half * 128 : half * 128 + 128]
                    out[:, 3 * h + k, ri, half] = part.reshape(8, 16, 128)


def point_kernel(field, weight, bias, out):
    w = jnp.concatenate([jnp.concatenate([weight[...]] * 8, axis=1)] * 8, axis=0)
    row = lax.broadcasted_iota(jnp.int32, (256, 256), 0) // 32
    col = lax.broadcasted_iota(jnp.int32, (256, 256), 1) // 32
    w = split(jnp.where(row == col, w, 0.0))
    b = jnp.concatenate([bias[...]] * 8, axis=0)
    for y in range(16):
        out[y] = (dot3(w, split(lines_at(field, y))) + b).reshape(2, 128, 128)


def z_back_kernel(rows, linear, table, out, work, sems):
    t = table[...]
    copies = []
    for i, (h, xs, ys) in enumerate(CHUNKS):
        by_y = jnp.swapaxes(rows[:, h, ys, :], 0, 1)
        cells = []
        for y in range(8):
            r = dot(jnp.concatenate(split(by_y[y]), axis=0).T, t)
            s = r[:, :128] + r[:, 128:] + linear[ys.start + y, h]
            cells.append(0.5 * s * (1.0 + lax.erf(s * np.float32(np.sqrt(0.5)))))
        cells = jnp.stack(cells)
        for x in range(4):
            at = (slice(None), 4 * h + x, ys)
            work[at] = jnp.swapaxes(cells[:, 32 * x : 32 * x + 32], 0, 1)
            copies.append(pltpu.make_async_copy(work.at[at], out.at[at], sems.at[4 * i + x]))
            copies[-1].start()
    for copy in copies:
        copy.wait()


VMEM = pl.BlockSpec(memory_space=pltpu.VMEM)
ANY = pl.BlockSpec(memory_space=pl.ANY)


def call(kernel, shape, *operands, ins=VMEM, outs=VMEM, scratch=(), limit=24, cost=None):
    return pl.pallas_call(
        kernel,
        out_shape=jax.ShapeDtypeStruct(shape, F32),
        in_specs=[ins] * len(operands),
        out_specs=outs,
        scratch_shapes=list(scratch),
        compiler_params=pltpu.CompilerParams(vmem_limit_bytes=limit * 1024 * 1024),
        cost_estimate=cost,
    )(*operands)


def exchange(v, axes):
    return lax.all_to_all(v, axes, 0, 0, tiled=True)


def on_device(field, weight, point_weight, point_bias):
    z_inv = z_inverse()
    y_fwd, y_inv = y_tables()
    x_fwd, x_inv = x_tables()
    block = pltpu.VMEM((C, 8, 16, NZ), F32)

    scratch = [block, pltpu.SemaphoreType.DMA((2,))]
    v = call(z_kernel, (96, 2, 16, 128), field, ins=ANY, scratch=scratch, limit=52)
    v = exchange(v.reshape(8, 12, 2, 16, 128), ("core", "px"))
    v = call(y_kernel, (1152, 128), v.reshape(8, 6, 2, 2, 16, 128), two(y_fwd))
    v = exchange(v.reshape(64, 9, 2, 128), GX + ("ph",))
    v = call(x_kernel, (256, 128), v.reshape(1152, 128), two(x_fwd))

    v, again = lax.optimization_barrier((v, field))
    bias = jnp.broadcast_to(point_bias[:, None], (C, NZ))
    cost = pl.CostEstimate(flops=800_000_000, bytes_accessed=4 << 20, transcendentals=0)
    linear = call(point_kernel, (16, 2, 128, 128), again.reshape(C * 8 * 16, NZ), point_weight.T, bias, cost=cost)
    v = exchange(v.reshape(32, 8, 128), ("zz", "yl"))
    v, linear = lax.optimization_barrier((v, linear))

    expand = np.kron(np.eye(C)[GX_OF], np.ones((1, C))).astype(ml_dtypes.bfloat16)
    scratch = [pltpu.VMEM((3, 96, 32), F32) for _ in range(4)]
    v = call(mix_kernel, (256, 128), v.reshape(256, 128), weight.transpose(0, 2, 1, 3), expand, scratch=scratch)

    v = exchange(v.reshape(32, 8, 128), ("zz", "yl"))
    v = call(x_back_kernel, (1152, 128), v.reshape(256, 128), two(x_inv))
    v = exchange(v.reshape(64, 9, 2, 128), GX + ("ph",))
    v = call(y_back_kernel, (8, 6, 2, 2, 16, 128), v.reshape(1152, 128), two(y_inv))
    v = exchange(v.reshape(8, 12, 2, 16, 128), ("core", "px"))
    hi, lo = two(z_inv)
    table = np.block([[hi, lo], [hi, np.zeros_like(lo)]])
    scratch = [block, pltpu.SemaphoreType.DMA((16,))]
    return call(
        z_back_kernel, (C, 8, 16, NZ), v.reshape(96, 2, 16, 128), linear, table, outs=ANY, scratch=scratch
    )


def solution(mesh):
    shape = (4, 8, 4, 2, 2)
    fine = Mesh(mesh.devices.reshape(shape), GX + GY)
    spec = P(None, GX, GY, None)
    return jax.shard_map(
        on_device,
        mesh=fine,
        in_specs=(spec, spec, P(), P()),
        out_specs=spec,
        check_vma=False,
    )
```

```python
import numpy as np

import jax
import jax.numpy as jnp
import ml_dtypes
from jax import lax
from jax.experimental import pallas as pl
from jax.experimental.pallas import tpu as pltpu
from jax.sharding import Mesh, PartitionSpec as P

F32 = jnp.float32
BF16 = jnp.bfloat16
GX = ("yl", "zz")
GY = ("px", "ph", "core")
C = 32
NX, NY, NZ = 256, 256, 128
M = 48
GX_OF = 8 * (np.arange(32) % 4) + np.arange(32) // 4
B = 64


def freq(i, kept=M):
    return np.where(i < kept // 2, i, i - kept)


def two(table):
    t = np.asarray(table, np.float32)
    hi = t.astype(ml_dtypes.bfloat16)
    lo = (t - hi.astype(np.float32)).astype(ml_dtypes.bfloat16)
    return np.stack([hi, lo])


def angle(f, pos, n):
    return 2.0 * np.pi * ((f * pos) % n) / n


def z_modes():
    d = np.arange(8)[:, None, None]
    h = np.arange(2)[None, :, None]
    k = np.arange(3)[None, None, :]
    return 3 * (4 * (d % 4) + 2 * h + d // 4) + k


def z_inverse():
    g = z_modes().reshape(-1)
    th = angle(g[:, None], np.arange(NZ)[None, :], NZ)
    w = (np.where(g == 0, 1.0, 2.0) / (NX * NY * NZ))[:, None]
    return np.stack([np.cos(th) * w, -np.sin(th) * w], axis=1).reshape(96, NZ)


def y_tables():
    f = freq(np.arange(M))
    d = np.arange(8)
    fwds, invs = [], []
    for h in range(2):
        pos = (64 * (d % 4) + 32 * h + 16 * (d // 4))[:, None] + np.arange(16)[None, :]
        th = angle(f[:, None], pos.reshape(1, -1), NY)
        cos, sin = np.zeros((B, 128)), np.zeros((B, 128))
        cos[:M], sin[:M] = np.cos(th), np.sin(th)
        fwds.append(np.block([[cos, sin], [-sin, cos]]))
        invs.append(np.block([[cos, sin], [-sin, cos]]).T)
    return np.stack(fwds), np.stack(invs)


def x_rows():
    gx = GX_OF
    first = 3 * (gx // 2) + gx % 2
    return np.stack([first, first + 1])


def x_tables():
    f = freq(x_rows().reshape(-1))
    pos = (8 * np.arange(32)[None, :] + np.arange(8)[:, None]).reshape(-1)
    th = angle(f[:, None], pos[None, :], NX)
    fwd = np.concatenate([np.cos(th), np.sin(th)])
    inv = np.concatenate([np.cos(th), np.sin(th)]).T
    return fwd, inv


def split(v):
    hi = v.astype(BF16)
    return hi, (v - hi.astype(F32)).astype(BF16)


def dot(a, b, dims=((1,), (0,))):
    return lax.dot_general(a, b, (dims, ((), ())), preferred_element_type=F32)


def dot3(a, b, dims=((1,), (0,))):
    return dot(a[0], b[0], dims) + dot(a[0], b[1], dims) + dot(a[1], b[0], dims)


NT = ((1,), (1,))


def lines_at(ref, y):
    return jnp.concatenate([ref[pl.ds(x * 16 + y, 32, stride=128), :] for x in range(8)], axis=0)


CHUNKS = [(h, slice(4 * h, 4 * h + 4), slice(8 * i, 8 * i + 8)) for h in range(2) for i in range(2)]


def z_table():
    m = lax.broadcasted_iota(jnp.int32, (96, NZ), 0).astype(F32)
    z = lax.broadcasted_iota(jnp.int32, (96, NZ), 1).astype(F32)
    d = jnp.floor((m + 0.5) * np.float32(1 / 12))
    j = jnp.floor((m - 12 * d + 0.5) * np.float32(1 / 2))
    ri = m - 12 * d - 2 * j
    q = jnp.floor(d * np.float32(1 / 4))
    h = jnp.floor((j + 0.5) * np.float32(1 / 3))
    g = 3 * (4 * (d - 4 * q) + 2 * h + q) + (j - 3 * h)
    turns = g * z + 32 * ri
    turns = turns - 128 * jnp.floor(turns * np.float32(1 / 128) + 0.5)
    return jnp.cos(turns * np.float32(2 * np.pi / 128))


def z_kernel(field, out, work, sems):
    copies = []
    for h in range(2):
        xs = slice(4 * h, 4 * h + 4)
        copies.append(pltpu.make_async_copy(field.at[:, xs], work.at[:, xs], sems.at[h]))
        copies[h].start()
    hi, lo = split(z_table())
    t = jnp.concatenate(
        [jnp.concatenate([hi, hi], axis=1), jnp.concatenate([lo, jnp.zeros_like(lo)], axis=1)], axis=0
    )
    for h, xs, ys in CHUNKS:
        if ys.start == 0:
            copies[h].wait()
        by_y = [jnp.swapaxes(work[:, 4 * h + x, ys, :], 0, 1) for x in range(4)]
        modes = []
        for y in range(8):
            a = jnp.concatenate([v[y] for v in by_y], axis=0)
            r = dot(t, jnp.concatenate(split(a), axis=1), NT)
            modes.append(r[:96] + r[96:])
        out[:, h, ys, :] = jnp.swapaxes(jnp.stack(modes), 0, 1)


def point(field, weight, bias, linear):
    w = jnp.concatenate([jnp.concatenate([weight[...]] * 8, axis=1)] * 8, axis=0)
    row = lax.broadcasted_iota(jnp.int32, (256, 256), 0) // 32
    col = lax.broadcasted_iota(jnp.int32, (256, 256), 1) // 32
    w = split(jnp.where(row == col, w, 0.0).T)
    b = jnp.broadcast_to(bias[...].reshape(1, 32), (NZ, 32)).T
    b = jnp.concatenate([b] * 8, axis=0)
    for y in range(16):
        linear[y] = (dot3(w, split(lines_at(field, y))) + b).reshape(2, 128, 128)


def y_kernel(rows, table, field, weight, bias, out, linear):
    half = lax.axis_index("ph")
    t = (table[0, half], table[1, half])
    for h in range(2):
        r = []
        for k in range(3):
            j = 3 * h + k
            b = jnp.concatenate(
                [
                    jnp.concatenate([rows[:, j, ri, half].reshape(128, 128) for ri in range(2)], axis=0)
                    for half in range(2)
                ],
                axis=1,
            )
            r.append(dot3(t, split(b)))
        for k in range(2):
            v = jnp.concatenate([r[k][:48], r[2][16 * k : 16 * k + 16], r[k][64:112], r[2][64 + 16 * k : 80 + 16 * k]], axis=0)
            v = v.T
            for x in range(8):
                out[pl.ds(h * 18 + k * 8 + x, 32, stride=36), :] = v[32 * x : 32 * x + 32]
        for xh in range(2):
            v = jnp.concatenate(
                [
                    r[2][64 * ri + 32 : 64 * ri + 48, 32 * x : 32 * x + 32]
                    for ri in range(2)
                    for x in range(4 * xh, 4 * xh + 4)
                ],
                axis=0,
            )
            out[pl.ds(h * 18 + 16 + xh, 32, stride=36), :] = v.T

    @pl.when(lax.axis_index("core") == 0)
    def _():
        point(field, weight, bias, linear)


def turn(v):
    rolled = pltpu.roll(v, B, 1)
    lane = lax.broadcasted_iota(jnp.int32, v.shape, 1)
    return jnp.where(lane < B, rolled, -rolled)


def x_kernel(rows, table, out):
    t = (table[0], table[1])
    at = lambda r: rows[pl.ds(r, 32, stride=36), :] + rows[pl.ds(18 + r, 32, stride=36), :]
    last = [at(16), at(17)]
    for k in range(3):
        if k < 2:
            s = [at(8 * k + x) for x in range(8)]
        else:
            s = [pltpu.roll(last[x // 4], (128 - 16 * (x % 4)) % 128, 1) for x in range(8)]
        r = dot3(t, split(jnp.concatenate(s, axis=0)))
        m = r[:64] + turn(r[64:])
        for a in range(2):
            out[pl.ds(2 * k + a, 32, stride=8), :] = m[32 * a : 32 * a + 32]
    for a in range(6, 8):
        out[pl.ds(a, 32, stride=8), :] = jnp.zeros((32, 128), F32)


def mix_kernel(modes, w, expand, out, in_re, in_im, mid_re, mid_im):
    start = pl.multiple_of(lax.axis_index("zz") % 2 * 24, 8)
    e = expand[...]
    for a in range(2):
        v = [modes[pl.ds(2 * k + a, 32, stride=8), :].T for k in range(3)]
        for ref, o in ((in_re, 0), (in_im, B)):
            for k in range(2):
                ref[k, a * 48 : a * 48 + 48, :] = v[k][o : o + 48]
                ref[2, a * 48 + 16 * k : a * 48 + 16 * k + 16, :] = v[k][o + 48 : o + 64]
            ref[2, a * 48 + 32 : a * 48 + 48, :] = v[2][o : o + 16]
    for k in range(3):
        mid_re[k] = jnp.zeros((96, 32), F32)
        mid_im[k] = jnp.zeros((96, 32), F32)
    for k in range(3):
        v = jnp.concatenate([in_re[k, pl.ds(start, 72), :], in_im[k, pl.ds(start, 72), :]], axis=0)
        hi, lo = split(v)
        wide = dot(hi, e) + dot(lo, e)
        re, im = wide[:72], wide[72:]
        w_re, w_im = w[0, k].astype(F32), w[1, k].astype(F32)
        for part, ref in ((re * w_re - im * w_im, mid_re), (re * w_im + im * w_re, mid_im)):
            s = part[:, 0:128]
            for i in range(1, 8):
                s = s + part[:, 128 * i : 128 * i + 128]
            s = s + pltpu.roll(s, 64, 1)
            s = s + pltpu.roll(s, 32, 1)
            ref[k, pl.ds(start, 72), :] = s[:, :32]
    pad = jnp.zeros((B - 16, 32), F32)
    for a in range(2):
        for k in range(3):
            v = []
            for ref in (mid_re, mid_im):
                if k < 2:
                    v += [ref[k, a * 48 : a * 48 + 48, :], ref[2, a * 48 + 16 * k : a * 48 + 16 * k + 16, :]]
                else:
                    v += [ref[2, a * 48 + 32 : a * 48 + 48, :], pad]
            v = jnp.concatenate(v, axis=0).T
            for yl in range(4):
                out[pl.ds(8 * yl + 2 * k + a, 8, stride=32), :] = v[8 * yl : 8 * yl + 8]
    for a in range(6, 8):
        out[pl.ds(a, 32, stride=8), :] = jnp.zeros((32, 128), F32)


def x_back_kernel(modes, table, out):
    t = (table[0], table[1])
    lane = lax.broadcasted_iota(jnp.int32, (32, 128), 1) % B
    for k in range(3):
        v = jnp.concatenate([modes[pl.ds(2 * k + a, 32, stride=8), :] for a in range(2)], axis=0)
        r = dot3(t, split(jnp.concatenate([v, -turn(v)], axis=0)))
        s = [r[32 * x : 32 * x + 32] for x in range(8)]
        if k == 2:
            packed = []
            for xh in range(2):
                v = s[4 * xh]
                for i in range(1, 4):
                    v = jnp.where(lane < 16 * i, v, pltpu.roll(s[4 * xh + i], 16 * i, 1))
                packed.append(v)
            s = packed
        for x in range(len(s)):
            for h in range(2):
                out[pl.ds(h * 18 + k * 8 + x, 32, stride=36), :] = s[x]


def y_back_kernel(rows, table, field, weight, bias, out, linear):
    half = lax.axis_index("ph")
    t = (table[0, half], table[1, half])
    lane = lax.broadcasted_iota(jnp.int32, (256, 128), 1) % B
    for h in range(2):
        at = lambda r: rows[pl.ds(h * 18 + r, 32, stride=36), :]
        v = [jnp.concatenate([at(8 * k + x) for x in range(8)], axis=0) for k in range(2)]
        last = [at(16), at(17)]
        v.append(
            jnp.concatenate([pltpu.roll(last[x // 4], (160 - 16 * (x % 4)) % 128, 1) for x in range(8)], axis=0)
        )
        v[2] = jnp.where(lane < 16, pltpu.roll(v[0], 80, 1), jnp.where(lane < 32, pltpu.roll(v[1], 96, 1), v[2]))
        for k in range(3):
            r = dot3(t, split(v[k]), NT)
            for ri in range(2):
                for half in range(2):
                    part = r[ri * 128 : ri * 128 + 128, half * 128 : half * 128 + 128]
                    out[:, 3 * h + k, ri, half] = part.reshape(8, 16, 128)

    @pl.when(lax.axis_index("core") == 1)
    def _():
        point(field, weight, bias, linear)


def z_back_kernel(rows, linear_0, linear_1, table, out, work, sems):
    t = table[...]
    first = lax.axis_index("core") == 0
    copies = []
    for i, (h, xs, ys) in enumerate(CHUNKS):
        by_y = jnp.swapaxes(rows[:, h, ys, :], 0, 1)
        cells = []
        for y in range(8):
            r = dot(jnp.concatenate(split(by_y[y]), axis=0).T, t)
            at = (ys.start + y, h)
            s = r[:, :128] + r[:, 128:] + jnp.where(first, linear_0[at], linear_1[at])
            cells.append(0.5 * s * (1.0 + lax.erf(s * np.float32(np.sqrt(0.5)))))
        cells = jnp.stack(cells)
        for x in range(4):
            at = (slice(None), 4 * h + x, ys)
            work[at] = jnp.swapaxes(cells[:, 32 * x : 32 * x + 32], 0, 1)
            copies.append(pltpu.make_async_copy(work.at[at], out.at[at], sems.at[4 * i + x]))
            copies[-1].start()
    for copy in copies:
        copy.wait()


VMEM = pl.BlockSpec(memory_space=pltpu.VMEM)
ANY = pl.BlockSpec(memory_space=pl.ANY)


def call(kernel, shape, *operands, ins=VMEM, outs=VMEM, scratch=(), limit=24):
    shapes = shape if isinstance(shape, list) else [shape]
    result = pl.pallas_call(
        kernel,
        out_shape=[jax.ShapeDtypeStruct(dims, F32) for dims in shapes],
        in_specs=[ins] * len(operands),
        out_specs=[outs] * len(shapes),
        scratch_shapes=list(scratch),
        compiler_params=pltpu.CompilerParams(vmem_limit_bytes=limit * 1024 * 1024),
    )(*operands)
    return result if isinstance(shape, list) else result[0]


def exchange(v, axes):
    return lax.all_to_all(v, axes, 0, 0, tiled=True)


def on_device(field, weight, point_weight, point_bias):
    z_inv = z_inverse()
    y_fwd, y_inv = y_tables()
    x_fwd, x_inv = x_tables()
    block = pltpu.VMEM((C, 8, 16, NZ), F32)

    scratch = [block, pltpu.SemaphoreType.DMA((2,))]
    v = call(z_kernel, (96, 2, 16, 128), field, ins=ANY, scratch=scratch, limit=52)
    v = exchange(v.reshape(8, 12, 2, 16, 128), ("core", "px"))
    lines = field.reshape(C * 8 * 16, NZ)
    mixing = (lines, point_weight, point_bias)
    mixed = (16, 2, 128, 128)
    v = v.reshape(8, 6, 2, 2, 16, 128)
    v, linear_0 = call(y_kernel, [(1152, 128), mixed], v, two(y_fwd), *mixing)
    v = exchange(v.reshape(64, 9, 2, 128), GX + ("ph",))
    v = call(x_kernel, (256, 128), v.reshape(1152, 128), two(x_fwd))

    v = exchange(v.reshape(32, 8, 128), ("zz", "yl"))

    expand = np.kron(np.eye(C)[GX_OF], np.ones((1, C))).astype(ml_dtypes.bfloat16)
    scratch = [pltpu.VMEM((3, 96, 32), F32) for _ in range(4)]
    v = call(mix_kernel, (256, 128), v.reshape(256, 128), weight.transpose(0, 2, 1, 3), expand, scratch=scratch)

    v = exchange(v.reshape(32, 8, 128), ("zz", "yl"))
    v = call(x_back_kernel, (1152, 128), v.reshape(256, 128), two(x_inv))
    v = exchange(v.reshape(64, 9, 2, 128), GX + ("ph",))
    v = v.reshape(1152, 128)
    v, linear_1 = call(y_back_kernel, [(8, 6, 2, 2, 16, 128), mixed], v, two(y_inv), *mixing)
    v = exchange(v.reshape(8, 12, 2, 16, 128), ("core", "px"))
    hi, lo = two(z_inv)
    table = np.block([[hi, lo], [hi, np.zeros_like(lo)]])
    scratch = [block, pltpu.SemaphoreType.DMA((16,))]
    v = v.reshape(96, 2, 16, 128)
    return call(z_back_kernel, (C, 8, 16, NZ), v, linear_0, linear_1, table, outs=ANY, scratch=scratch)


def solution(mesh):
    shape = (4, 8, 4, 2, 2)
    fine = Mesh(mesh.devices.reshape(shape), GX + GY)
    spec = P(None, GX, GY, None)
    return jax.shard_map(
        on_device,
        mesh=fine,
        in_specs=(spec, spec, P(), P()),
        out_specs=spec,
        check_vma=False,
    )
```

```python
import numpy as np

import jax
import jax.numpy as jnp
import ml_dtypes
from jax import lax
from jax.experimental import pallas as pl
from jax.experimental.pallas import tpu as pltpu
from jax.sharding import Mesh, PartitionSpec as P

F32 = jnp.float32
BF16 = jnp.bfloat16
GX = ("yl", "zz")
GY = ("px", "ph", "core")
C = 32
NX, NY, NZ = 256, 256, 128
M = 48
GX_OF = 8 * (np.arange(32) % 4) + np.arange(32) // 4
B = 64


def freq(i, kept=M):
    return np.where(i < kept // 2, i, i - kept)


def two(table):
    t = np.asarray(table, np.float32)
    hi = t.astype(ml_dtypes.bfloat16)
    lo = (t - hi.astype(np.float32)).astype(ml_dtypes.bfloat16)
    return np.stack([hi, lo])


def angle(f, pos, n):
    return 2.0 * np.pi * ((f * pos) % n) / n


def z_modes():
    d = np.arange(8)[:, None, None]
    h = np.arange(2)[None, :, None]
    k = np.arange(3)[None, None, :]
    return 3 * (4 * (d % 4) + 2 * h + d // 4) + k


def z_inverse():
    g = z_modes().reshape(-1)
    th = angle(g[:, None], np.arange(NZ)[None, :], NZ)
    w = (np.where(g == 0, 1.0, 2.0) / (NX * NY * NZ))[:, None]
    return np.stack([np.cos(th) * w, -np.sin(th) * w], axis=1).reshape(96, NZ)


def y_tables():
    f = freq(np.arange(M))
    d = np.arange(8)
    fwds, invs = [], []
    for h in range(2):
        pos = (64 * (d % 4) + 32 * h + 16 * (d // 4))[:, None] + np.arange(16)[None, :]
        th = angle(f[:, None], pos.reshape(1, -1), NY)
        cos, sin = np.zeros((B, 128)), np.zeros((B, 128))
        cos[:M], sin[:M] = np.cos(th), np.sin(th)
        fwds.append(np.block([[cos, sin], [-sin, cos]]))
        invs.append(np.block([[cos, sin], [-sin, cos]]).T)
    return np.stack(fwds), np.stack(invs)


def x_rows():
    gx = GX_OF
    first = 3 * (gx // 2) + gx % 2
    return np.stack([first, first + 1])


def x_tables():
    f = freq(x_rows().reshape(-1))
    pos = (8 * GX_OF[None, :] + np.arange(8)[:, None]).reshape(-1)
    th = angle(f[:, None], pos[None, :], NX)
    fwd = np.concatenate([np.cos(th), np.sin(th)])
    inv = np.concatenate([np.cos(th), np.sin(th)]).T
    return fwd, inv


def split(v):
    hi = v.astype(BF16)
    return hi, (v - hi.astype(F32)).astype(BF16)


def dot(a, b, dims=((1,), (0,))):
    return lax.dot_general(a, b, (dims, ((), ())), preferred_element_type=F32)


def dot3(a, b, dims=((1,), (0,))):
    return dot(a[0], b[0], dims) + dot(a[0], b[1], dims) + dot(a[1], b[0], dims)


NT = ((1,), (1,))


def lines_at(ref, y):
    return jnp.concatenate([ref[pl.ds(x * 16 + y, 32, stride=128), :] for x in range(8)], axis=0)


CHUNKS = [(h, slice(4 * h, 4 * h + 4), slice(8 * i, 8 * i + 8)) for h in range(2) for i in range(2)]


def z_table():
    m = lax.broadcasted_iota(jnp.int32, (96, NZ), 0).astype(F32)
    z = lax.broadcasted_iota(jnp.int32, (96, NZ), 1).astype(F32)
    d = jnp.floor((m + 0.5) * np.float32(1 / 12))
    j = jnp.floor((m - 12 * d + 0.5) * np.float32(1 / 2))
    ri = m - 12 * d - 2 * j
    q = jnp.floor(d * np.float32(1 / 4))
    h = jnp.floor((j + 0.5) * np.float32(1 / 3))
    g = 3 * (4 * (d - 4 * q) + 2 * h + q) + (j - 3 * h)
    turns = g * z + 32 * ri
    turns = turns - 128 * jnp.floor(turns * np.float32(1 / 128) + 0.5)
    return jnp.cos(turns * np.float32(2 * np.pi / 128))


def z_kernel(field, out, work, sems):
    copies = []
    for h in range(2):
        xs = slice(4 * h, 4 * h + 4)
        copies.append(pltpu.make_async_copy(field.at[:, xs], work.at[:, xs], sems.at[h]))
        copies[h].start()
    hi, lo = split(z_table())
    t = jnp.concatenate(
        [jnp.concatenate([hi, hi], axis=1), jnp.concatenate([lo, jnp.zeros_like(lo)], axis=1)], axis=0
    )
    for h, xs, ys in CHUNKS:
        if ys.start == 0:
            copies[h].wait()
        by_y = [jnp.swapaxes(work[:, 4 * h + x, ys, :], 0, 1) for x in range(4)]
        modes = []
        for y in range(8):
            a = jnp.concatenate([v[y] for v in by_y], axis=0)
            r = dot(t, jnp.concatenate(split(a), axis=1), NT)
            modes.append(r[:96] + r[96:])
        out[:, h, ys, :] = jnp.swapaxes(jnp.stack(modes), 0, 1)


def point(field, weight, bias, linear):
    w = jnp.concatenate([jnp.concatenate([weight[...]] * 8, axis=1)] * 8, axis=0)
    row = lax.broadcasted_iota(jnp.int32, (256, 256), 0) // 32
    col = lax.broadcasted_iota(jnp.int32, (256, 256), 1) // 32
    w = split(jnp.where(row == col, w, 0.0).T)
    b = jnp.broadcast_to(bias[...].reshape(1, 32), (NZ, 32)).T
    b = jnp.concatenate([b] * 8, axis=0)
    for y in range(16):
        linear[y] = (dot3(w, split(lines_at(field, y))) + b).reshape(2, 128, 128)


def y_kernel(rows, table, field, weight, bias, out, linear):
    half = lax.axis_index("ph")
    t = (table[0, half], table[1, half])
    for h in range(2):
        r = []
        for k in range(3):
            j = 3 * h + k
            b = jnp.concatenate(
                [
                    jnp.concatenate([rows[:, j, ri, half].reshape(128, 128) for ri in range(2)], axis=0)
                    for half in range(2)
                ],
                axis=1,
            )
            r.append(dot3(t, split(b)))
        for k in range(2):
            v = jnp.concatenate([r[k][:48], r[2][16 * k : 16 * k + 16], r[k][64:112], r[2][64 + 16 * k : 80 + 16 * k]], axis=0)
            v = v.T
            for x in range(8):
                out[pl.ds(h * 576 + k * 8 + x, 32, stride=18), :] = v[32 * x : 32 * x + 32]
        for xh in range(2):
            v = jnp.concatenate(
                [
                    r[2][64 * ri + 32 : 64 * ri + 48, 32 * x : 32 * x + 32]
                    for ri in range(2)
                    for x in range(4 * xh, 4 * xh + 4)
                ],
                axis=0,
            )
            out[pl.ds(h * 576 + 16 + xh, 32, stride=18), :] = v.T

    @pl.when(lax.axis_index("core") == 0)
    def _():
        point(field, weight, bias, linear)


def turn(v):
    rolled = pltpu.roll(v, B, 1)
    lane = lax.broadcasted_iota(jnp.int32, v.shape, 1)
    return jnp.where(lane < B, rolled, -rolled)


def x_kernel(rows, table, out):
    t = (table[0], table[1])
    at = lambda r: rows[pl.ds(r, 32, stride=18), :] + rows[pl.ds(576 + r, 32, stride=18), :]
    last = [at(16), at(17)]
    for k in range(3):
        if k < 2:
            s = [at(8 * k + x) for x in range(8)]
        else:
            s = [pltpu.roll(last[x // 4], (128 - 16 * (x % 4)) % 128, 1) for x in range(8)]
        r = dot3(t, split(jnp.concatenate(s, axis=0)))
        m = r[:64] + turn(r[64:])
        for a in range(2):
            out[pl.ds(2 * k + a, 32, stride=6), :] = m[32 * a : 32 * a + 32]


def mix_kernel(modes, w, expand, out, in_re, in_im, mid_re, mid_im):
    start = pl.multiple_of(lax.axis_index("zz") % 2 * 24, 8)
    e = expand[...]
    for a in range(2):
        v = [modes[pl.ds(2 * k + a, 32, stride=6), :].T for k in range(3)]
        for ref, o in ((in_re, 0), (in_im, B)):
            for k in range(2):
                ref[k, a * 48 : a * 48 + 48, :] = v[k][o : o + 48]
                ref[2, a * 48 + 16 * k : a * 48 + 16 * k + 16, :] = v[k][o + 48 : o + 64]
            ref[2, a * 48 + 32 : a * 48 + 48, :] = v[2][o : o + 16]
    for k in range(3):
        mid_re[k] = jnp.zeros((96, 32), F32)
        mid_im[k] = jnp.zeros((96, 32), F32)
    for k in range(3):
        v = jnp.concatenate([in_re[k, pl.ds(start, 72), :], in_im[k, pl.ds(start, 72), :]], axis=0)
        hi, lo = split(v)
        wide = dot(hi, e) + dot(lo, e)
        re, im = wide[:72], wide[72:]
        w_re, w_im = w[0, k].astype(F32), w[1, k].astype(F32)
        for part, ref in ((re * w_re - im * w_im, mid_re), (re * w_im + im * w_re, mid_im)):
            s = part[:, 0:128]
            for i in range(1, 8):
                s = s + part[:, 128 * i : 128 * i + 128]
            s = s + pltpu.roll(s, 64, 1)
            s = s + pltpu.roll(s, 32, 1)
            ref[k, pl.ds(start, 72), :] = s[:, :32]
    pad = jnp.zeros((B - 16, 32), F32)
    for a in range(2):
        for k in range(3):
            v = []
            for ref in (mid_re, mid_im):
                if k < 2:
                    v += [ref[k, a * 48 : a * 48 + 48, :], ref[2, a * 48 + 16 * k : a * 48 + 16 * k + 16, :]]
                else:
                    v += [ref[2, a * 48 + 32 : a * 48 + 48, :], pad]
            v = jnp.concatenate(v, axis=0).T
            out[pl.ds(2 * k + a, 32, stride=6), :] = v


def x_back_kernel(modes, table, out):
    t = (table[0], table[1])
    lane = lax.broadcasted_iota(jnp.int32, (32, 128), 1) % B
    for k in range(3):
        v = jnp.concatenate([modes[pl.ds(2 * k + a, 32, stride=6), :] for a in range(2)], axis=0)
        r = dot3(t, split(jnp.concatenate([v, -turn(v)], axis=0)))
        s = [r[32 * x : 32 * x + 32] for x in range(8)]
        if k == 2:
            packed = []
            for xh in range(2):
                v = s[4 * xh]
                for i in range(1, 4):
                    v = jnp.where(lane < 16 * i, v, pltpu.roll(s[4 * xh + i], 16 * i, 1))
                packed.append(v)
            s = packed
        for x in range(len(s)):
            for h in range(2):
                out[pl.ds(h * 576 + k * 8 + x, 32, stride=18), :] = s[x]


def y_back_kernel(rows, table, field, weight, bias, out, linear):
    half = lax.axis_index("ph")
    t = (table[0, half], table[1, half])
    lane = lax.broadcasted_iota(jnp.int32, (256, 128), 1) % B
    for h in range(2):
        at = lambda r: rows[pl.ds(h * 576 + r, 32, stride=18), :]
        v = [jnp.concatenate([at(8 * k + x) for x in range(8)], axis=0) for k in range(2)]
        last = [at(16), at(17)]
        v.append(
            jnp.concatenate([pltpu.roll(last[x // 4], (160 - 16 * (x % 4)) % 128, 1) for x in range(8)], axis=0)
        )
        v[2] = jnp.where(lane < 16, pltpu.roll(v[0], 80, 1), jnp.where(lane < 32, pltpu.roll(v[1], 96, 1), v[2]))
        for k in range(3):
            r = dot3(t, split(v[k]), NT)
            for ri in range(2):
                for half in range(2):
                    part = r[ri * 128 : ri * 128 + 128, half * 128 : half * 128 + 128]
                    out[:, 3 * h + k, ri, half] = part.reshape(8, 16, 128)

    @pl.when(lax.axis_index("core") == 1)
    def _():
        point(field, weight, bias, linear)


def z_back_kernel(rows, linear_0, linear_1, table, out, work, sems):
    t = table[...]
    first = lax.axis_index("core") == 0
    copies = []
    for i, (h, xs, ys) in enumerate(CHUNKS):
        by_y = jnp.swapaxes(rows[:, h, ys, :], 0, 1)
        cells = []
        for y in range(8):
            r = dot(jnp.concatenate(split(by_y[y]), axis=0).T, t)
            at = (ys.start + y, h)
            s = r[:, :128] + r[:, 128:] + jnp.where(first, linear_0[at], linear_1[at])
            cells.append(0.5 * s * (1.0 + lax.erf(s * np.float32(np.sqrt(0.5)))))
        cells = jnp.stack(cells)
        for x in range(4):
            at = (slice(None), 4 * h + x, ys)
            work[at] = jnp.swapaxes(cells[:, 32 * x : 32 * x + 32], 0, 1)
            copies.append(pltpu.make_async_copy(work.at[at], out.at[at], sems.at[4 * i + x]))
            copies[-1].start()
    for copy in copies:
        copy.wait()


VMEM = pl.BlockSpec(memory_space=pltpu.VMEM)
ANY = pl.BlockSpec(memory_space=pl.ANY)


def call(kernel, shape, *operands, ins=VMEM, outs=VMEM, scratch=(), limit=24):
    shapes = shape if isinstance(shape, list) else [shape]
    result = pl.pallas_call(
        kernel,
        out_shape=[jax.ShapeDtypeStruct(dims, F32) for dims in shapes],
        in_specs=[ins] * len(operands),
        out_specs=[outs] * len(shapes),
        scratch_shapes=list(scratch),
        compiler_params=pltpu.CompilerParams(vmem_limit_bytes=limit * 1024 * 1024),
    )(*operands)
    return result if isinstance(shape, list) else result[0]


def exchange(v, axes):
    return lax.all_to_all(v, axes, 0, 0, tiled=True)


def on_device(field, weight, point_weight, point_bias):
    z_inv = z_inverse()
    y_fwd, y_inv = y_tables()
    x_fwd, x_inv = x_tables()
    block = pltpu.VMEM((C, 8, 16, NZ), F32)

    scratch = [block, pltpu.SemaphoreType.DMA((2,))]
    v = call(z_kernel, (96, 2, 16, 128), field, ins=ANY, scratch=scratch, limit=52)
    v = exchange(v.reshape(8, 12, 2, 16, 128), ("core", "px"))
    lines = field.reshape(C * 8 * 16, NZ)
    mixing = (lines, point_weight, point_bias)
    mixed = (16, 2, 128, 128)
    v = v.reshape(8, 6, 2, 2, 16, 128)
    v, linear_0 = call(y_kernel, [(1152, 128), mixed], v, two(y_fwd), *mixing)
    v = exchange(v.reshape(64, 9, 2, 128), ("ph", "zz", "yl"))
    v = call(x_kernel, (192, 128), v.reshape(1152, 128), two(x_fwd))

    v = exchange(v.reshape(32, 3, 2, 128), ("zz", "yl"))

    expand = np.kron(np.eye(C), np.ones((1, C))).astype(ml_dtypes.bfloat16)
    scratch = [pltpu.VMEM((3, 96, 32), F32) for _ in range(4)]
    v = call(mix_kernel, (192, 128), v.reshape(192, 128), weight.transpose(0, 2, 1, 3), expand, scratch=scratch)

    v = exchange(v.reshape(32, 3, 2, 128), ("zz", "yl"))
    v = call(x_back_kernel, (1152, 128), v.reshape(192, 128), two(x_inv))
    v = exchange(v.reshape(64, 9, 2, 128), ("ph", "zz", "yl"))
    v = v.reshape(1152, 128)
    v, linear_1 = call(y_back_kernel, [(8, 6, 2, 2, 16, 128), mixed], v, two(y_inv), *mixing)
    v = exchange(v.reshape(8, 12, 2, 16, 128), ("core", "px"))
    hi, lo = two(z_inv)
    table = np.block([[hi, lo], [hi, np.zeros_like(lo)]])
    scratch = [block, pltpu.SemaphoreType.DMA((16,))]
    v = v.reshape(96, 2, 16, 128)
    return call(z_back_kernel, (C, 8, 16, NZ), v, linear_0, linear_1, table, outs=ANY, scratch=scratch)


def solution(mesh):
    shape = (4, 8, 4, 2, 2)
    fine = Mesh(mesh.devices.reshape(shape), GX + GY)
    spec = P(None, GX, GY, None)
    return jax.shard_map(
        on_device,
        mesh=fine,
        in_specs=(spec, spec, P(), P()),
        out_specs=spec,
        check_vma=False,
    )
```

```python
import numpy as np

import jax
import jax.numpy as jnp
import ml_dtypes
from jax import lax
from jax.experimental import pallas as pl
from jax.experimental.pallas import tpu as pltpu
from jax.sharding import Mesh, PartitionSpec as P

F32 = jnp.float32
BF16 = jnp.bfloat16
GX = ("yl", "zz")
GY = ("px", "ph", "core")
C = 32
NX, NY, NZ = 256, 256, 128
M = 48
GX_OF = 8 * (np.arange(32) % 4) + np.arange(32) // 4
B = 64


def freq(i, kept=M):
    return np.where(i < kept // 2, i, i - kept)


def two(table):
    t = np.asarray(table, np.float32)
    hi = t.astype(ml_dtypes.bfloat16)
    lo = (t - hi.astype(np.float32)).astype(ml_dtypes.bfloat16)
    return np.stack([hi, lo])


def angle(f, pos, n):
    return 2.0 * np.pi * ((f * pos) % n) / n


def z_modes():
    d = np.arange(8)[:, None, None]
    h = np.arange(2)[None, :, None]
    k = np.arange(3)[None, None, :]
    return 3 * (4 * (d % 4) + 2 * h + d // 4) + k


def z_inverse():
    g = z_modes().reshape(-1)
    th = angle(g[:, None], np.arange(NZ)[None, :], NZ)
    w = (np.where(g == 0, 1.0, 2.0) / (NX * NY * NZ))[:, None]
    return np.stack([np.cos(th) * w, -np.sin(th) * w], axis=1).reshape(96, NZ)


def y_tables():
    f = freq(np.arange(M))
    d = np.arange(8)
    fwds, invs = [], []
    for h in range(2):
        pos = (64 * (d % 4) + 32 * h + 16 * (d // 4))[:, None] + np.arange(16)[None, :]
        th = angle(f[:, None], pos.reshape(1, -1), NY)
        cos, sin = np.zeros((B, 128)), np.zeros((B, 128))
        cos[:M], sin[:M] = np.cos(th), np.sin(th)
        fwds.append(np.block([[cos, sin], [-sin, cos]]))
        invs.append(np.block([[cos, sin], [-sin, cos]]).T)
    return np.stack(fwds), np.stack(invs)


def x_rows():
    gx = GX_OF
    first = 3 * (gx // 2) + gx % 2
    return np.stack([first, first + 1])


def x_tables():
    f = freq(x_rows().reshape(-1))
    pos = (8 * GX_OF[None, :] + np.arange(8)[:, None]).reshape(-1)
    th = angle(f[:, None], pos[None, :], NX)
    fwd = np.concatenate([np.cos(th), np.sin(th)])
    inv = np.concatenate([np.cos(th), np.sin(th)]).T
    return fwd, inv


def split(v):
    hi = v.astype(BF16)
    return hi, (v - hi.astype(F32)).astype(BF16)


def dot(a, b, dims=((1,), (0,))):
    return lax.dot_general(a, b, (dims, ((), ())), preferred_element_type=F32)


def dot3(a, b, dims=((1,), (0,))):
    return dot(a[0], b[0], dims) + dot(a[0], b[1], dims) + dot(a[1], b[0], dims)


NT = ((1,), (1,))


CHUNKS = [(h, slice(4 * h, 4 * h + 4), slice(8 * i, 8 * i + 8)) for h in range(2) for i in range(2)]


def z_table():
    m = lax.broadcasted_iota(jnp.int32, (96, NZ), 0).astype(F32)
    z = lax.broadcasted_iota(jnp.int32, (96, NZ), 1).astype(F32)
    d = jnp.floor((m + 0.5) * np.float32(1 / 12))
    j = jnp.floor((m - 12 * d + 0.5) * np.float32(1 / 2))
    ri = m - 12 * d - 2 * j
    q = jnp.floor(d * np.float32(1 / 4))
    h = jnp.floor((j + 0.5) * np.float32(1 / 3))
    g = 3 * (4 * (d - 4 * q) + 2 * h + q) + (j - 3 * h)
    turns = g * z + 32 * ri
    turns = turns - 128 * jnp.floor(turns * np.float32(1 / 128) + 0.5)
    return jnp.cos(turns * np.float32(2 * np.pi / 128))


def z_kernel(field, out, work, sems):
    copies = []
    for h in range(2):
        xs = slice(4 * h, 4 * h + 4)
        copies.append(pltpu.make_async_copy(field.at[:, xs], work.at[:, xs], sems.at[h]))
        copies[h].start()
    hi, lo = split(z_table())
    t = jnp.concatenate(
        [jnp.concatenate([hi, hi], axis=1), jnp.concatenate([lo, jnp.zeros_like(lo)], axis=1)], axis=0
    )
    for h, xs, ys in CHUNKS:
        if ys.start == 0:
            copies[h].wait()
        by_y = [jnp.swapaxes(work[:, 4 * h + x, ys, :], 0, 1) for x in range(4)]
        modes = []
        for y in range(8):
            a = jnp.concatenate([v[y] for v in by_y], axis=0)
            r = dot(t, jnp.concatenate(split(a), axis=1), NT)
            modes.append(r[:96] + r[96:])
        out[:, h, ys, :] = jnp.swapaxes(jnp.stack(modes), 0, 1)


def point(field, weight, bias, linear):
    w = jnp.concatenate([jnp.concatenate([weight[...]] * 8, axis=1)] * 8, axis=0)
    row = lax.broadcasted_iota(jnp.int32, (256, 256), 0) // 32
    col = lax.broadcasted_iota(jnp.int32, (256, 256), 1) // 32
    w = split(jnp.where(row == col, w, 0.0).T)
    b = jnp.broadcast_to(bias[...].reshape(1, 32), (NZ, 32)).T
    b = jnp.concatenate([b] * 8, axis=0)
    for i in range(2):
        by_y = [jnp.swapaxes(field[:, x, 8 * i : 8 * i + 8, :], 0, 1) for x in range(8)]
        for y in range(8):
            hi, lo = split(jnp.concatenate([v[y] for v in by_y], axis=0))
            r = dot(w[0], jnp.concatenate([hi, lo], axis=1))
            r = r[:, :NZ] + r[:, NZ:] + dot(w[1], hi) + b
            linear[8 * i + y] = r.reshape(2, 128, 128)


def y_kernel(rows, table, field, weight, bias, out, linear):
    half = lax.axis_index("ph")
    t = (table[0, half], table[1, half])
    for h in range(2):
        r = []
        for k in range(3):
            j = 3 * h + k
            b = jnp.concatenate(
                [
                    jnp.concatenate([rows[:, j, ri, half].reshape(128, 128) for ri in range(2)], axis=0)
                    for half in range(2)
                ],
                axis=1,
            )
            r.append(dot3(t, split(b)))
        for k in range(2):
            v = jnp.concatenate([r[k][:48], r[2][16 * k : 16 * k + 16], r[k][64:112], r[2][64 + 16 * k : 80 + 16 * k]], axis=0)
            v = v.T
            for x in range(8):
                out[pl.ds(h * 576 + k * 8 + x, 32, stride=18), :] = v[32 * x : 32 * x + 32]
        for xh in range(2):
            v = jnp.concatenate(
                [
                    r[2][64 * ri + 32 : 64 * ri + 48, 32 * x : 32 * x + 32]
                    for ri in range(2)
                    for x in range(4 * xh, 4 * xh + 4)
                ],
                axis=0,
            )
            out[pl.ds(h * 576 + 16 + xh, 32, stride=18), :] = v.T

    @pl.when(lax.axis_index("core") == 0)
    def _():
        point(field, weight, bias, linear)


def turn(v):
    rolled = pltpu.roll(v, B, 1)
    lane = lax.broadcasted_iota(jnp.int32, v.shape, 1)
    return jnp.where(lane < B, rolled, -rolled)


def x_kernel(rows, table, out):
    t = (table[0], table[1])
    at = lambda r: rows[pl.ds(r, 32, stride=18), :] + rows[pl.ds(576 + r, 32, stride=18), :]
    last = [at(16), at(17)]
    for k in range(3):
        if k < 2:
            s = [at(8 * k + x) for x in range(8)]
        else:
            s = [pltpu.roll(last[x // 4], (128 - 16 * (x % 4)) % 128, 1) for x in range(8)]
        r = dot3(t, split(jnp.concatenate(s, axis=0)))
        m = r[:64] + turn(r[64:])
        for a in range(2):
            out[pl.ds(2 * k + a, 32, stride=6), :] = m[32 * a : 32 * a + 32]


def mix_kernel(modes, w, expand, out, in_re, in_im, mid_re, mid_im):
    start = pl.multiple_of(lax.axis_index("zz") % 2 * 24, 8)
    e = expand[...]
    for a in range(2):
        v = [modes[pl.ds(2 * k + a, 32, stride=6), :].T for k in range(3)]
        for ref, o in ((in_re, 0), (in_im, B)):
            for k in range(2):
                ref[k, a * 48 : a * 48 + 48, :] = v[k][o : o + 48]
                ref[2, a * 48 + 16 * k : a * 48 + 16 * k + 16, :] = v[k][o + 48 : o + 64]
            ref[2, a * 48 + 32 : a * 48 + 48, :] = v[2][o : o + 16]
    for k in range(3):
        mid_re[k] = jnp.zeros((96, 32), F32)
        mid_im[k] = jnp.zeros((96, 32), F32)
    for k in range(3):
        v = jnp.concatenate([in_re[k, pl.ds(start, 72), :], in_im[k, pl.ds(start, 72), :]], axis=0)
        hi, lo = split(v)
        wide = dot(hi, e) + dot(lo, e)
        re, im = wide[:72], wide[72:]
        w_re, w_im = w[0, k].astype(F32), w[1, k].astype(F32)
        for part, ref in ((re * w_re - im * w_im, mid_re), (re * w_im + im * w_re, mid_im)):
            s = part[:, 0:128]
            for i in range(1, 8):
                s = s + part[:, 128 * i : 128 * i + 128]
            s = s + pltpu.roll(s, 64, 1)
            s = s + pltpu.roll(s, 32, 1)
            ref[k, pl.ds(start, 72), :] = s[:, :32]
    pad = jnp.zeros((B - 16, 32), F32)
    for a in range(2):
        for k in range(3):
            v = []
            for ref in (mid_re, mid_im):
                if k < 2:
                    v += [ref[k, a * 48 : a * 48 + 48, :], ref[2, a * 48 + 16 * k : a * 48 + 16 * k + 16, :]]
                else:
                    v += [ref[2, a * 48 + 32 : a * 48 + 48, :], pad]
            v = jnp.concatenate(v, axis=0).T
            out[pl.ds(2 * k + a, 32, stride=6), :] = v


def x_back_kernel(modes, table, out):
    t = (table[0], table[1])
    lane = lax.broadcasted_iota(jnp.int32, (32, 128), 1) % B
    for k in range(3):
        v = jnp.concatenate([modes[pl.ds(2 * k + a, 32, stride=6), :] for a in range(2)], axis=0)
        r = dot3(t, split(jnp.concatenate([v, -turn(v)], axis=0)))
        s = [r[32 * x : 32 * x + 32] for x in range(8)]
        if k == 2:
            packed = []
            for xh in range(2):
                v = s[4 * xh]
                for i in range(1, 4):
                    v = jnp.where(lane < 16 * i, v, pltpu.roll(s[4 * xh + i], 16 * i, 1))
                packed.append(v)
            s = packed
        for x in range(len(s)):
            for h in range(2):
                out[pl.ds(h * 576 + k * 8 + x, 32, stride=18), :] = s[x]


def y_back_kernel(rows, table, field, weight, bias, out, linear):
    half = lax.axis_index("ph")
    t = (table[0, half], table[1, half])
    lane = lax.broadcasted_iota(jnp.int32, (256, 128), 1) % B
    for h in range(2):
        at = lambda r: rows[pl.ds(h * 576 + r, 32, stride=18), :]
        v = [jnp.concatenate([at(8 * k + x) for x in range(8)], axis=0) for k in range(2)]
        last = [at(16), at(17)]
        v.append(
            jnp.concatenate([pltpu.roll(last[x // 4], (160 - 16 * (x % 4)) % 128, 1) for x in range(8)], axis=0)
        )
        v[2] = jnp.where(lane < 16, pltpu.roll(v[0], 80, 1), jnp.where(lane < 32, pltpu.roll(v[1], 96, 1), v[2]))
        for k in range(3):
            r = dot3(t, split(v[k]), NT)
            for ri in range(2):
                for half in range(2):
                    part = r[ri * 128 : ri * 128 + 128, half * 128 : half * 128 + 128]
                    out[:, 3 * h + k, ri, half] = part.reshape(8, 16, 128)

    @pl.when(lax.axis_index("core") == 1)
    def _():
        point(field, weight, bias, linear)


def z_back_kernel(rows, linear_0, linear_1, table, out, work, sems):
    t = table[...]
    first = lax.axis_index("core") == 0
    copies = []
    for i, (h, xs, ys) in enumerate(CHUNKS):
        by_y = jnp.swapaxes(rows[:, h, ys, :], 0, 1)
        cells = []
        for y in range(8):
            r = dot(jnp.concatenate(split(by_y[y]), axis=0).T, t)
            at = (ys.start + y, h)
            s = r[:, :128] + r[:, 128:] + jnp.where(first, linear_0[at], linear_1[at])
            cells.append(0.5 * s * (1.0 + lax.erf(s * np.float32(np.sqrt(0.5)))))
        cells = jnp.stack(cells)
        for x in range(4):
            at = (slice(None), 4 * h + x, ys)
            work[at] = jnp.swapaxes(cells[:, 32 * x : 32 * x + 32], 0, 1)
            copies.append(pltpu.make_async_copy(work.at[at], out.at[at], sems.at[4 * i + x]))
            copies[-1].start()
    for copy in copies:
        copy.wait()


VMEM = pl.BlockSpec(memory_space=pltpu.VMEM)
ANY = pl.BlockSpec(memory_space=pl.ANY)


def call(kernel, shape, *operands, ins=VMEM, outs=VMEM, scratch=(), limit=24):
    shapes = shape if isinstance(shape, list) else [shape]
    result = pl.pallas_call(
        kernel,
        out_shape=[jax.ShapeDtypeStruct(dims, F32) for dims in shapes],
        in_specs=[ins] * len(operands),
        out_specs=[outs] * len(shapes),
        scratch_shapes=list(scratch),
        compiler_params=pltpu.CompilerParams(vmem_limit_bytes=limit * 1024 * 1024),
    )(*operands)
    return result if isinstance(shape, list) else result[0]


def exchange(v, axes):
    return lax.all_to_all(v, axes, 0, 0, tiled=True)


def on_device(field, weight, point_weight, point_bias):
    z_inv = z_inverse()
    y_fwd, y_inv = y_tables()
    x_fwd, x_inv = x_tables()
    block = pltpu.VMEM((C, 8, 16, NZ), F32)

    scratch = [block, pltpu.SemaphoreType.DMA((2,))]
    v = call(z_kernel, (96, 2, 16, 128), field, ins=ANY, scratch=scratch, limit=52)
    v = exchange(v.reshape(8, 12, 2, 16, 128), ("core", "px"))
    mixing = (field, point_weight, point_bias)
    mixed = (16, 2, 128, 128)
    v = v.reshape(8, 6, 2, 2, 16, 128)
    v, linear_0 = call(y_kernel, [(1152, 128), mixed], v, two(y_fwd), *mixing)
    v = exchange(v.reshape(64, 9, 2, 128), ("ph", "zz", "yl"))
    v = call(x_kernel, (192, 128), v.reshape(1152, 128), two(x_fwd))

    v = exchange(v.reshape(32, 3, 2, 128), ("zz", "yl"))

    expand = np.kron(np.eye(C), np.ones((1, C))).astype(ml_dtypes.bfloat16)
    scratch = [pltpu.VMEM((3, 96, 32), F32) for _ in range(4)]
    v = call(mix_kernel, (192, 128), v.reshape(192, 128), weight.transpose(0, 2, 1, 3), expand, scratch=scratch)

    v = exchange(v.reshape(32, 3, 2, 128), ("zz", "yl"))
    v = call(x_back_kernel, (1152, 128), v.reshape(192, 128), two(x_inv))
    v = exchange(v.reshape(64, 9, 2, 128), ("ph", "zz", "yl"))
    v = v.reshape(1152, 128)
    v, linear_1 = call(y_back_kernel, [(8, 6, 2, 2, 16, 128), mixed], v, two(y_inv), *mixing)
    v = exchange(v.reshape(8, 12, 2, 16, 128), ("core", "px"))
    hi, lo = two(z_inv)
    table = np.block([[hi, lo], [hi, np.zeros_like(lo)]])
    scratch = [block, pltpu.SemaphoreType.DMA((16,))]
    v = v.reshape(96, 2, 16, 128)
    return call(z_back_kernel, (C, 8, 16, NZ), v, linear_0, linear_1, table, outs=ANY, scratch=scratch)


def solution(mesh):
    shape = (4, 8, 4, 2, 2)
    fine = Mesh(mesh.devices.reshape(shape), GX + GY)
    spec = P(None, GX, GY, None)
    return jax.shard_map(
        on_device,
        mesh=fine,
        in_specs=(spec, spec, P(), P()),
        out_specs=spec,
        check_vma=False,
    )
```

```python
import numpy as np

import jax
import jax.numpy as jnp
import ml_dtypes
from jax import lax
from jax.experimental import pallas as pl
from jax.experimental.pallas import tpu as pltpu
from jax.sharding import Mesh, PartitionSpec as P

F32 = jnp.float32
BF16 = jnp.bfloat16
GX = ("yl", "zz")
GY = ("px", "ph", "core")
C = 32
NX, NY, NZ = 256, 256, 128
M = 48
GX_OF = 8 * (np.arange(32) % 4) + np.arange(32) // 4
B = 64


def freq(i, kept=M):
    return np.where(i < kept // 2, i, i - kept)


def two(table):
    t = np.asarray(table, np.float32)
    hi = t.astype(ml_dtypes.bfloat16)
    lo = (t - hi.astype(np.float32)).astype(ml_dtypes.bfloat16)
    return np.stack([hi, lo])


def angle(f, pos, n):
    return 2.0 * np.pi * ((f * pos) % n) / n


def z_modes():
    d = np.arange(8)[:, None, None]
    h = np.arange(2)[None, :, None]
    k = np.arange(3)[None, None, :]
    return 3 * (4 * (d % 4) + 2 * h + d // 4) + k


def z_inverse():
    g = z_modes().reshape(-1)
    th = angle(g[:, None], np.arange(NZ)[None, :], NZ)
    w = (np.where(g == 0, 1.0, 2.0) / (NX * NY * NZ))[:, None]
    return np.stack([np.cos(th) * w, -np.sin(th) * w], axis=1).reshape(96, NZ)


def y_tables():
    f = freq(np.arange(M))
    d = np.arange(8)
    fwds, invs = [], []
    for h in range(2):
        pos = (64 * (d % 4) + 32 * h + 16 * (d // 4))[:, None] + np.arange(16)[None, :]
        th = angle(f[:, None], pos.reshape(1, -1), NY)
        cos, sin = np.zeros((B, 128)), np.zeros((B, 128))
        cos[:M], sin[:M] = np.cos(th), np.sin(th)
        fwds.append(np.block([[cos, sin], [-sin, cos]]))
        invs.append(np.block([[cos, sin], [-sin, cos]]).T)
    return np.stack(fwds), np.stack(invs)


def x_rows():
    gx = np.arange(32)
    first = 3 * (gx // 2) + gx % 2
    return np.stack([first, first + 1])


def x_tables():
    f = freq(x_rows().reshape(-1))
    pos = (8 * GX_OF[None, :] + np.arange(8)[:, None]).reshape(-1)
    th = angle(f[:, None], pos[None, :], NX)
    fwd = np.concatenate([np.cos(th), np.sin(th)])
    inv = np.concatenate([np.cos(th), np.sin(th)]).T
    return fwd, inv


def split(v):
    hi = v.astype(BF16)
    return hi, (v - hi.astype(F32)).astype(BF16)


def dot(a, b, dims=((1,), (0,))):
    return lax.dot_general(a, b, (dims, ((), ())), preferred_element_type=F32)


def dot3(a, b, dims=((1,), (0,))):
    return dot(a[0], b[0], dims) + dot(a[0], b[1], dims) + dot(a[1], b[0], dims)


NT = ((1,), (1,))


def lines_at(ref, y):
    return jnp.concatenate([ref[pl.ds(x * 16 + y, 32, stride=128), :] for x in range(8)], axis=0)


CHUNKS = [(h, slice(4 * h, 4 * h + 4), slice(8 * i, 8 * i + 8)) for h in range(2) for i in range(2)]


def z_table():
    m = lax.broadcasted_iota(jnp.int32, (96, NZ), 0).astype(F32)
    z = lax.broadcasted_iota(jnp.int32, (96, NZ), 1).astype(F32)
    d = jnp.floor((m + 0.5) * np.float32(1 / 12))
    j = jnp.floor((m - 12 * d + 0.5) * np.float32(1 / 2))
    ri = m - 12 * d - 2 * j
    q = jnp.floor(d * np.float32(1 / 4))
    h = jnp.floor((j + 0.5) * np.float32(1 / 3))
    g = 3 * (4 * (d - 4 * q) + 2 * h + q) + (j - 3 * h)
    turns = g * z + 32 * ri
    turns = turns - 128 * jnp.floor(turns * np.float32(1 / 128) + 0.5)
    return jnp.cos(turns * np.float32(2 * np.pi / 128))


def z_kernel(field, out, work, sems):
    copies = []
    for h in range(2):
        xs = slice(4 * h, 4 * h + 4)
        copies.append(pltpu.make_async_copy(field.at[:, xs], work.at[:, xs], sems.at[h]))
        copies[h].start()
    hi, lo = split(z_table())
    t = jnp.concatenate(
        [jnp.concatenate([hi, hi], axis=1), jnp.concatenate([lo, jnp.zeros_like(lo)], axis=1)], axis=0
    )
    for h, xs, ys in CHUNKS:
        if ys.start == 0:
            copies[h].wait()
        by_y = [jnp.swapaxes(work[:, 4 * h + x, ys, :], 0, 1) for x in range(4)]
        modes = []
        for y in range(8):
            a = jnp.concatenate([v[y] for v in by_y], axis=0)
            r = dot(t, jnp.concatenate(split(a), axis=1), NT)
            modes.append(r[:96] + r[96:])
        out[:, h, ys, :] = jnp.swapaxes(jnp.stack(modes), 0, 1)


def point(field, weight, bias, linear):
    w = jnp.concatenate([jnp.concatenate([weight[...]] * 8, axis=1)] * 8, axis=0)
    row = lax.broadcasted_iota(jnp.int32, (256, 256), 0) // 32
    col = lax.broadcasted_iota(jnp.int32, (256, 256), 1) // 32
    w = split(jnp.where(row == col, w, 0.0).T)
    b = jnp.broadcast_to(bias[...].reshape(1, 32), (NZ, 32)).T
    b = jnp.concatenate([b] * 8, axis=0)
    for y in range(16):
        linear[y] = (dot3(w, split(lines_at(field, y))) + b).reshape(2, 128, 128)


def y_kernel(rows, table, field, weight, bias, out, linear):
    half = lax.axis_index("ph")
    t = (table[0, half], table[1, half])
    for h in range(2):
        r = []
        for k in range(3):
            j = 3 * h + k
            b = jnp.concatenate(
                [
                    jnp.concatenate([rows[:, j, ri, half].reshape(128, 128) for ri in range(2)], axis=0)
                    for half in range(2)
                ],
                axis=1,
            )
            r.append(dot3(t, split(b)))
        for k in range(2):
            v = jnp.concatenate([r[k][:48], r[2][16 * k : 16 * k + 16], r[k][64:112], r[2][64 + 16 * k : 80 + 16 * k]], axis=0)
            v = v.T
            for x in range(8):
                out[pl.ds(h * 576 + k * 8 + x, 32, stride=18), :] = v[32 * x : 32 * x + 32]
        for xh in range(2):
            v = jnp.concatenate(
                [
                    r[2][64 * ri + 32 : 64 * ri + 48, 32 * x : 32 * x + 32]
                    for ri in range(2)
                    for x in range(4 * xh, 4 * xh + 4)
                ],
                axis=0,
            )
            out[pl.ds(h * 576 + 16 + xh, 32, stride=18), :] = v.T

    @pl.when(lax.axis_index("core") == 0)
    def _():
        point(field, weight, bias, linear)


def turn(v):
    rolled = pltpu.roll(v, B, 1)
    lane = lax.broadcasted_iota(jnp.int32, v.shape, 1)
    return jnp.where(lane < B, rolled, -rolled)


def x_kernel(rows, table, out):
    t = (table[0], table[1])
    at = lambda r: rows[pl.ds(r, 32, stride=18), :] + rows[pl.ds(576 + r, 32, stride=18), :]
    last = [at(16), at(17)]
    for k in range(3):
        if k < 2:
            s = [at(8 * k + x) for x in range(8)]
        else:
            s = [pltpu.roll(last[x // 4], (128 - 16 * (x % 4)) % 128, 1) for x in range(8)]
        r = dot3(t, split(jnp.concatenate(s, axis=0)))
        m = r[:64] + turn(r[64:])
        for a in range(2):
            out[pl.ds(2 * k + a, 32, stride=6), :] = m[32 * a : 32 * a + 32]


def mix_kernel(modes, w, expand, out, in_re, in_im, mid_re, mid_im):
    start = pl.multiple_of(lax.axis_index("zz") % 2 * 24, 8)
    e = expand[...]
    for a in range(2):
        v = [modes[pl.ds(2 * k + a, 32, stride=6), :].T for k in range(3)]
        for ref, o in ((in_re, 0), (in_im, B)):
            for k in range(2):
                ref[k, a * 48 : a * 48 + 48, :] = v[k][o : o + 48]
                ref[2, a * 48 + 16 * k : a * 48 + 16 * k + 16, :] = v[k][o + 48 : o + 64]
            ref[2, a * 48 + 32 : a * 48 + 48, :] = v[2][o : o + 16]
    for k in range(3):
        mid_re[k] = jnp.zeros((96, 32), F32)
        mid_im[k] = jnp.zeros((96, 32), F32)
    for k in range(3):
        v = jnp.concatenate([in_re[k, pl.ds(start, 72), :], in_im[k, pl.ds(start, 72), :]], axis=0)
        hi, lo = split(v)
        wide = dot(hi, e) + dot(lo, e)
        re, im = wide[:72], wide[72:]
        w_re, w_im = w[0, k].astype(F32), w[1, k].astype(F32)
        for part, ref in ((re * w_re - im * w_im, mid_re), (re * w_im + im * w_re, mid_im)):
            s = part[:, 0:128]
            for i in range(1, 8):
                s = s + part[:, 128 * i : 128 * i + 128]
            s = s + pltpu.roll(s, 64, 1)
            s = s + pltpu.roll(s, 32, 1)
            ref[k, pl.ds(start, 72), :] = s[:, :32]
    pad = jnp.zeros((B - 16, 32), F32)
    for a in range(2):
        for k in range(3):
            v = []
            for ref in (mid_re, mid_im):
                if k < 2:
                    v += [ref[k, a * 48 : a * 48 + 48, :], ref[2, a * 48 + 16 * k : a * 48 + 16 * k + 16, :]]
                else:
                    v += [ref[2, a * 48 + 32 : a * 48 + 48, :], pad]
            v = jnp.concatenate(v, axis=0).T
            for zz in range(8):
                out[pl.ds(6 * zz + 2 * k + a, 4, stride=48), :] = v[4 * zz : 4 * zz + 4]


def x_back_kernel(modes, table, out):
    t = (table[0], table[1])
    lane = lax.broadcasted_iota(jnp.int32, (32, 128), 1) % B
    for k in range(3):
        v = jnp.concatenate([modes[pl.ds(2 * k + a, 32, stride=6), :] for a in range(2)], axis=0)
        r = dot3(t, split(jnp.concatenate([v, -turn(v)], axis=0)))
        s = [r[32 * x : 32 * x + 32] for x in range(8)]
        if k == 2:
            packed = []
            for xh in range(2):
                v = s[4 * xh]
                for i in range(1, 4):
                    v = jnp.where(lane < 16 * i, v, pltpu.roll(s[4 * xh + i], 16 * i, 1))
                packed.append(v)
            s = packed
        for x in range(len(s)):
            for h in range(2):
                out[pl.ds(h * 576 + k * 8 + x, 32, stride=18), :] = s[x]


def y_back_kernel(rows, table, field, weight, bias, out, linear):
    half = lax.axis_index("ph")
    t = (table[0, half], table[1, half])
    lane = lax.broadcasted_iota(jnp.int32, (256, 128), 1) % B
    for h in range(2):
        at = lambda r: rows[pl.ds(h * 576 + r, 32, stride=18), :]
        v = [jnp.concatenate([at(8 * k + x) for x in range(8)], axis=0) for k in range(2)]
        last = [at(16), at(17)]
        v.append(
            jnp.concatenate([pltpu.roll(last[x // 4], (160 - 16 * (x % 4)) % 128, 1) for x in range(8)], axis=0)
        )
        v[2] = jnp.where(lane < 16, pltpu.roll(v[0], 80, 1), jnp.where(lane < 32, pltpu.roll(v[1], 96, 1), v[2]))
        for k in range(3):
            r = dot3(t, split(v[k]), NT)
            for ri in range(2):
                for half in range(2):
                    part = r[ri * 128 : ri * 128 + 128, half * 128 : half * 128 + 128]
                    out[:, 3 * h + k, ri, half] = part.reshape(8, 16, 128)

    @pl.when(lax.axis_index("core") == 1)
    def _():
        point(field, weight, bias, linear)


def z_back_kernel(rows, linear_0, linear_1, table, out, work, sems):
    t = table[...]
    first = lax.axis_index("core") == 0
    copies = []
    for i, (h, xs, ys) in enumerate(CHUNKS):
        by_y = jnp.swapaxes(rows[:, h, ys, :], 0, 1)
        cells = []
        for y in range(8):
            r = dot(jnp.concatenate(split(by_y[y]), axis=0).T, t)
            at = (ys.start + y, h)
            s = r[:, :128] + r[:, 128:] + jnp.where(first, linear_0[at], linear_1[at])
            cells.append(0.5 * s * (1.0 + lax.erf(s * np.float32(np.sqrt(0.5)))))
        cells = jnp.stack(cells)
        for x in range(4):
            at = (slice(None), 4 * h + x, ys)
            work[at] = jnp.swapaxes(cells[:, 32 * x : 32 * x + 32], 0, 1)
            copies.append(pltpu.make_async_copy(work.at[at], out.at[at], sems.at[4 * i + x]))
            copies[-1].start()
    for copy in copies:
        copy.wait()


VMEM = pl.BlockSpec(memory_space=pltpu.VMEM)
ANY = pl.BlockSpec(memory_space=pl.ANY)


def call(kernel, shape, *operands, ins=VMEM, outs=VMEM, scratch=(), limit=24):
    shapes = shape if isinstance(shape, list) else [shape]
    result = pl.pallas_call(
        kernel,
        out_shape=[jax.ShapeDtypeStruct(dims, F32) for dims in shapes],
        in_specs=[ins] * len(operands),
        out_specs=[outs] * len(shapes),
        scratch_shapes=list(scratch),
        compiler_params=pltpu.CompilerParams(vmem_limit_bytes=limit * 1024 * 1024),
    )(*operands)
    return result if isinstance(shape, list) else result[0]


def exchange(v, axes):
    return lax.all_to_all(v, axes, 0, 0, tiled=True)


def on_device(field, weight, point_weight, point_bias):
    z_inv = z_inverse()
    y_fwd, y_inv = y_tables()
    x_fwd, x_inv = x_tables()
    block = pltpu.VMEM((C, 8, 16, NZ), F32)

    scratch = [block, pltpu.SemaphoreType.DMA((2,))]
    v = call(z_kernel, (96, 2, 16, 128), field, ins=ANY, scratch=scratch, limit=52)
    v = exchange(v.reshape(8, 12, 2, 16, 128), ("core", "px"))
    lines = field.reshape(C * 8 * 16, NZ)
    mixing = (lines, point_weight, point_bias)
    mixed = (16, 2, 128, 128)
    v = v.reshape(8, 6, 2, 2, 16, 128)
    v, linear_0 = call(y_kernel, [(1152, 128), mixed], v, two(y_fwd), *mixing)
    v = exchange(v.reshape(64, 9, 2, 128), ("ph", "zz", "yl"))
    v = call(x_kernel, (192, 128), v.reshape(1152, 128), two(x_fwd))

    v = exchange(v.reshape(32, 3, 2, 128), GX)

    expand = np.kron(np.eye(C)[np.argsort(GX_OF)], np.ones((1, C))).astype(ml_dtypes.bfloat16)
    scratch = [pltpu.VMEM((3, 96, 32), F32) for _ in range(4)]
    v = call(mix_kernel, (192, 128), v.reshape(192, 128), weight.transpose(0, 2, 1, 3), expand, scratch=scratch)

    v = exchange(v.reshape(32, 3, 2, 128), GX)
    v = call(x_back_kernel, (1152, 128), v.reshape(192, 128), two(x_inv))
    v = exchange(v.reshape(64, 9, 2, 128), ("ph", "zz", "yl"))
    v = v.reshape(1152, 128)
    v, linear_1 = call(y_back_kernel, [(8, 6, 2, 2, 16, 128), mixed], v, two(y_inv), *mixing)
    v = exchange(v.reshape(8, 12, 2, 16, 128), ("core", "px"))
    hi, lo = two(z_inv)
    table = np.block([[hi, lo], [hi, np.zeros_like(lo)]])
    scratch = [block, pltpu.SemaphoreType.DMA((16,))]
    v = v.reshape(96, 2, 16, 128)
    return call(z_back_kernel, (C, 8, 16, NZ), v, linear_0, linear_1, table, outs=ANY, scratch=scratch)


def solution(mesh):
    shape = (4, 8, 4, 2, 2)
    fine = Mesh(mesh.devices.reshape(shape), GX + GY)
    spec = P(None, GX, GY, None)
    return jax.shard_map(
        on_device,
        mesh=fine,
        in_specs=(spec, spec, P(), P()),
        out_specs=spec,
        check_vma=False,
    )
```

```python
import numpy as np

import jax
import jax.numpy as jnp
import ml_dtypes
from jax import lax
from jax.experimental import pallas as pl
from jax.experimental.pallas import tpu as pltpu
from jax.sharding import Mesh, PartitionSpec as P

F32 = jnp.float32
BF16 = jnp.bfloat16
GX = ("yl", "zz")
GY = ("px", "ph", "core")
C = 32
NX, NY, NZ = 256, 256, 128
M = 48
GX_OF = 8 * (np.arange(32) % 4) + np.arange(32) // 4
B = 64


def freq(i, kept=M):
    return np.where(i < kept // 2, i, i - kept)


def two(table):
    t = np.asarray(table, np.float32)
    hi = t.astype(ml_dtypes.bfloat16)
    lo = (t - hi.astype(np.float32)).astype(ml_dtypes.bfloat16)
    return np.stack([hi, lo])


def angle(f, pos, n):
    return 2.0 * np.pi * ((f * pos) % n) / n


def z_modes():
    d = np.arange(8)[:, None, None]
    h = np.arange(2)[None, :, None]
    k = np.arange(3)[None, None, :]
    return 3 * (4 * (d % 4) + 2 * h + d // 4) + k


def z_inverse():
    g = z_modes().reshape(-1)
    th = angle(g[:, None], np.arange(NZ)[None, :], NZ)
    w = (np.where(g == 0, 1.0, 2.0) / (NX * NY * NZ))[:, None]
    return np.stack([np.cos(th) * w, -np.sin(th) * w], axis=1).reshape(96, NZ)


def y_tables():
    f = freq(np.arange(M))
    d = np.arange(8)
    fwds, invs = [], []
    for h in range(2):
        pos = (64 * (d % 4) + 32 * h + 16 * (d // 4))[:, None] + np.arange(16)[None, :]
        th = angle(f[:, None], pos.reshape(1, -1), NY)
        cos, sin = np.zeros((B, 128)), np.zeros((B, 128))
        cos[:M], sin[:M] = np.cos(th), np.sin(th)
        fwds.append(np.block([[cos, sin], [-sin, cos]]))
        invs.append(np.block([[cos, sin], [-sin, cos]]).T)
    return np.stack(fwds), np.stack(invs)


def x_rows():
    gx = np.arange(32)
    first = 3 * (gx // 2) + gx % 2
    return np.stack([first, first + 1])


def x_tables():
    f = freq(x_rows().reshape(-1))
    pos = (8 * GX_OF[None, :] + np.arange(8)[:, None]).reshape(-1)
    th = angle(f[:, None], pos[None, :], NX)
    fwd = np.concatenate([np.cos(th), np.sin(th)])
    inv = np.concatenate([np.cos(th), np.sin(th)]).T
    return fwd, inv


def split(v):
    hi = v.astype(BF16)
    return hi, (v - hi.astype(F32)).astype(BF16)


def dot(a, b, dims=((1,), (0,))):
    return lax.dot_general(a, b, (dims, ((), ())), preferred_element_type=F32)


def dot3(a, b, dims=((1,), (0,))):
    return dot(a[0], b[0], dims) + dot(a[0], b[1], dims) + dot(a[1], b[0], dims)


NT = ((1,), (1,))


CHUNKS = [(h, slice(4 * h, 4 * h + 4), slice(8 * i, 8 * i + 8)) for h in range(2) for i in range(2)]


def z_table():
    m = lax.broadcasted_iota(jnp.int32, (96, NZ), 0).astype(F32)
    z = lax.broadcasted_iota(jnp.int32, (96, NZ), 1).astype(F32)
    d = jnp.floor((m + 0.5) * np.float32(1 / 12))
    j = jnp.floor((m - 12 * d + 0.5) * np.float32(1 / 2))
    ri = m - 12 * d - 2 * j
    q = jnp.floor(d * np.float32(1 / 4))
    h = jnp.floor((j + 0.5) * np.float32(1 / 3))
    g = 3 * (4 * (d - 4 * q) + 2 * h + q) + (j - 3 * h)
    turns = g * z + 32 * ri
    turns = turns - 128 * jnp.floor(turns * np.float32(1 / 128) + 0.5)
    return jnp.cos(turns * np.float32(2 * np.pi / 128))


def z_kernel(field, out, work, sems):
    copies = []
    for h in range(2):
        xs = slice(4 * h, 4 * h + 4)
        copies.append(pltpu.make_async_copy(field.at[:, xs], work.at[:, xs], sems.at[h]))
        copies[h].start()
    hi, lo = split(z_table())
    t = jnp.concatenate(
        [jnp.concatenate([hi, hi], axis=1), jnp.concatenate([lo, jnp.zeros_like(lo)], axis=1)], axis=0
    )
    for h, xs, ys in CHUNKS:
        if ys.start == 0:
            copies[h].wait()
        by_y = [jnp.swapaxes(work[:, 4 * h + x, ys, :], 0, 1) for x in range(4)]
        modes = []
        for y in range(8):
            a = jnp.concatenate([v[y] for v in by_y], axis=0)
            r = dot(t, jnp.concatenate(split(a), axis=1), NT)
            modes.append(r[:96] + r[96:])
        out[:, h, ys, :] = jnp.swapaxes(jnp.stack(modes), 0, 1)


def point(field, weight, bias, linear):
    w = jnp.concatenate([jnp.concatenate([weight[...]] * 8, axis=1)] * 8, axis=0)
    row = lax.broadcasted_iota(jnp.int32, (256, 256), 0) // 32
    col = lax.broadcasted_iota(jnp.int32, (256, 256), 1) // 32
    w = split(jnp.where(row == col, w, 0.0).T)
    b = jnp.broadcast_to(bias[...].reshape(1, 32), (NZ, 32)).T
    b = jnp.concatenate([b] * 8, axis=0)
    for i in range(2):
        by_y = [jnp.swapaxes(field[:, x, 8 * i : 8 * i + 8, :], 0, 1) for x in range(8)]
        for y in range(8):
            hi, lo = split(jnp.concatenate([v[y] for v in by_y], axis=0))
            r = dot(w[0], jnp.concatenate([hi, lo], axis=1))
            r = r[:, :NZ] + r[:, NZ:] + dot(w[1], hi) + b
            linear[8 * i + y] = r.reshape(2, 128, 128)


def y_kernel(rows, table, field, weight, bias, out, linear):
    half = lax.axis_index("ph")
    t = (table[0, half], table[1, half])
    for h in range(2):
        r = []
        for k in range(3):
            j = 3 * h + k
            b = jnp.concatenate(
                [
                    jnp.concatenate([rows[:, j, ri, half].reshape(128, 128) for ri in range(2)], axis=0)
                    for half in range(2)
                ],
                axis=1,
            )
            r.append(dot3(t, split(b)))
        for k in range(2):
            v = jnp.concatenate([r[k][:48], r[2][16 * k : 16 * k + 16], r[k][64:112], r[2][64 + 16 * k : 80 + 16 * k]], axis=0)
            v = v.T
            for x in range(8):
                out[pl.ds(h * 576 + k * 8 + x, 32, stride=18), :] = v[32 * x : 32 * x + 32]
        for xh in range(2):
            v = jnp.concatenate(
                [
                    r[2][64 * ri + 32 : 64 * ri + 48, 32 * x : 32 * x + 32]
                    for ri in range(2)
                    for x in range(4 * xh, 4 * xh + 4)
                ],
                axis=0,
            )
            out[pl.ds(h * 576 + 16 + xh, 32, stride=18), :] = v.T

    @pl.when(lax.axis_index("core") == 0)
    def _():
        point(field, weight, bias, linear)


def turn(v):
    rolled = pltpu.roll(v, B, 1)
    lane = lax.broadcasted_iota(jnp.int32, v.shape, 1)
    return jnp.where(lane < B, rolled, -rolled)


def x_kernel(rows, table, out):
    t = (table[0], table[1])
    at = lambda r: rows[pl.ds(r, 32, stride=18), :] + rows[pl.ds(576 + r, 32, stride=18), :]
    last = [at(16), at(17)]
    for k in range(3):
        if k < 2:
            s = [at(8 * k + x) for x in range(8)]
        else:
            s = [pltpu.roll(last[x // 4], (128 - 16 * (x % 4)) % 128, 1) for x in range(8)]
        r = dot3(t, split(jnp.concatenate(s, axis=0)))
        m = r[:64] + turn(r[64:])
        for a in range(2):
            out[pl.ds(2 * k + a, 32, stride=6), :] = m[32 * a : 32 * a + 32]


def mix_kernel(modes, w, expand, out, in_re, in_im, mid_re, mid_im):
    start = pl.multiple_of(lax.axis_index("zz") % 2 * 24, 8)
    e = expand[...]
    for a in range(2):
        v = [modes[pl.ds(2 * k + a, 32, stride=6), :].T for k in range(3)]
        for ref, o in ((in_re, 0), (in_im, B)):
            for k in range(2):
                ref[k, a * 48 : a * 48 + 48, :] = v[k][o : o + 48]
                ref[2, a * 48 + 16 * k : a * 48 + 16 * k + 16, :] = v[k][o + 48 : o + 64]
            ref[2, a * 48 + 32 : a * 48 + 48, :] = v[2][o : o + 16]
    for k in range(3):
        mid_re[k] = jnp.zeros((96, 32), F32)
        mid_im[k] = jnp.zeros((96, 32), F32)
    for k in range(3):
        v = jnp.concatenate([in_re[k, pl.ds(start, 72), :], in_im[k, pl.ds(start, 72), :]], axis=0)
        hi, lo = split(v)
        wide = dot(hi, e) + dot(lo, e)
        re, im = wide[:72], wide[72:]
        w_re, w_im = w[0, k].astype(F32), w[1, k].astype(F32)
        for part, ref in ((re * w_re - im * w_im, mid_re), (re * w_im + im * w_re, mid_im)):
            s = part[:, 0:128]
            for i in range(1, 8):
                s = s + part[:, 128 * i : 128 * i + 128]
            s = s + pltpu.roll(s, 64, 1)
            s = s + pltpu.roll(s, 32, 1)
            ref[k, pl.ds(start, 72), :] = s[:, :32]
    pad = jnp.zeros((B - 16, 32), F32)
    for a in range(2):
        for k in range(3):
            v = []
            for ref in (mid_re, mid_im):
                if k < 2:
                    v += [ref[k, a * 48 : a * 48 + 48, :], ref[2, a * 48 + 16 * k : a * 48 + 16 * k + 16, :]]
                else:
                    v += [ref[2, a * 48 + 32 : a * 48 + 48, :], pad]
            v = jnp.concatenate(v, axis=0).T
            for zz in range(8):
                out[pl.ds(6 * zz + 2 * k + a, 4, stride=48), :] = v[4 * zz : 4 * zz + 4]


def x_back_kernel(modes, table, out):
    t = (table[0], table[1])
    lane = lax.broadcasted_iota(jnp.int32, (32, 128), 1) % B
    for k in range(3):
        v = jnp.concatenate([modes[pl.ds(2 * k + a, 32, stride=6), :] for a in range(2)], axis=0)
        r = dot3(t, split(jnp.concatenate([v, -turn(v)], axis=0)))
        s = [r[32 * x : 32 * x + 32] for x in range(8)]
        if k == 2:
            packed = []
            for xh in range(2):
                v = s[4 * xh]
                for i in range(1, 4):
                    v = jnp.where(lane < 16 * i, v, pltpu.roll(s[4 * xh + i], 16 * i, 1))
                packed.append(v)
            s = packed
        for x in range(len(s)):
            for h in range(2):
                out[pl.ds(h * 576 + k * 8 + x, 32, stride=18), :] = s[x]


def y_back_kernel(rows, table, field, weight, bias, out, linear):
    half = lax.axis_index("ph")
    t = (table[0, half], table[1, half])
    lane = lax.broadcasted_iota(jnp.int32, (256, 128), 1) % B
    for h in range(2):
        at = lambda r: rows[pl.ds(h * 576 + r, 32, stride=18), :]
        v = [jnp.concatenate([at(8 * k + x) for x in range(8)], axis=0) for k in range(2)]
        last = [at(16), at(17)]
        v.append(
            jnp.concatenate([pltpu.roll(last[x // 4], (160 - 16 * (x % 4)) % 128, 1) for x in range(8)], axis=0)
        )
        v[2] = jnp.where(lane < 16, pltpu.roll(v[0], 80, 1), jnp.where(lane < 32, pltpu.roll(v[1], 96, 1), v[2]))
        for k in range(3):
            r = dot3(t, split(v[k]), NT)
            for ri in range(2):
                for half in range(2):
                    part = r[ri * 128 : ri * 128 + 128, half * 128 : half * 128 + 128]
                    out[:, 3 * h + k, ri, half] = part.reshape(8, 16, 128)

    @pl.when(lax.axis_index("core") == 1)
    def _():
        point(field, weight, bias, linear)


def z_back_kernel(rows, linear_0, linear_1, table, out, work, sems):
    t = table[...]
    first = lax.axis_index("core") == 0
    copies = []
    for i, (h, xs, ys) in enumerate(CHUNKS):
        by_y = jnp.swapaxes(rows[:, h, ys, :], 0, 1)
        cells = []
        for y in range(8):
            r = dot(jnp.concatenate(split(by_y[y]), axis=0).T, t)
            at = (ys.start + y, h)
            s = r[:, :128] + r[:, 128:] + jnp.where(first, linear_0[at], linear_1[at])
            cells.append(0.5 * s * (1.0 + lax.erf(s * np.float32(np.sqrt(0.5)))))
        cells = jnp.stack(cells)
        for x in range(4):
            at = (slice(None), 4 * h + x, ys)
            work[at] = jnp.swapaxes(cells[:, 32 * x : 32 * x + 32], 0, 1)
            copies.append(pltpu.make_async_copy(work.at[at], out.at[at], sems.at[4 * i + x]))
            copies[-1].start()
    for copy in copies:
        copy.wait()


VMEM = pl.BlockSpec(memory_space=pltpu.VMEM)
ANY = pl.BlockSpec(memory_space=pl.ANY)


def call(kernel, shape, *operands, ins=VMEM, outs=VMEM, scratch=(), limit=24):
    shapes = shape if isinstance(shape, list) else [shape]
    result = pl.pallas_call(
        kernel,
        out_shape=[jax.ShapeDtypeStruct(dims, F32) for dims in shapes],
        in_specs=[ins] * len(operands),
        out_specs=[outs] * len(shapes),
        scratch_shapes=list(scratch),
        compiler_params=pltpu.CompilerParams(vmem_limit_bytes=limit * 1024 * 1024),
    )(*operands)
    return result if isinstance(shape, list) else result[0]


def exchange(v, axes):
    return lax.all_to_all(v, axes, 0, 0, tiled=True)


def on_device(field, weight, point_weight, point_bias):
    z_inv = z_inverse()
    y_fwd, y_inv = y_tables()
    x_fwd, x_inv = x_tables()
    block = pltpu.VMEM((C, 8, 16, NZ), F32)

    scratch = [block, pltpu.SemaphoreType.DMA((2,))]
    v = call(z_kernel, (96, 2, 16, 128), field, ins=ANY, scratch=scratch, limit=52)
    v = exchange(v.reshape(8, 12, 2, 16, 128), ("core", "px"))
    mixing = (field, point_weight, point_bias)
    mixed = (16, 2, 128, 128)
    v = v.reshape(8, 6, 2, 2, 16, 128)
    v, linear_0 = call(y_kernel, [(1152, 128), mixed], v, two(y_fwd), *mixing)
    v = exchange(v.reshape(64, 9, 2, 128), ("ph", "zz", "yl"))
    v = call(x_kernel, (192, 128), v.reshape(1152, 128), two(x_fwd))

    v = exchange(v.reshape(32, 3, 2, 128), GX)

    expand = np.kron(np.eye(C)[np.argsort(GX_OF)], np.ones((1, C))).astype(ml_dtypes.bfloat16)
    scratch = [pltpu.VMEM((3, 96, 32), F32) for _ in range(4)]
    v = call(mix_kernel, (192, 128), v.reshape(192, 128), weight.transpose(0, 2, 1, 3), expand, scratch=scratch)

    v = exchange(v.reshape(32, 3, 2, 128), GX)
    v = call(x_back_kernel, (1152, 128), v.reshape(192, 128), two(x_inv))
    v = exchange(v.reshape(64, 9, 2, 128), ("ph", "zz", "yl"))
    v = v.reshape(1152, 128)
    v, linear_1 = call(y_back_kernel, [(8, 6, 2, 2, 16, 128), mixed], v, two(y_inv), *mixing)
    v = exchange(v.reshape(8, 12, 2, 16, 128), ("core", "px"))
    hi, lo = two(z_inv)
    table = np.block([[hi, lo], [hi, np.zeros_like(lo)]])
    scratch = [block, pltpu.SemaphoreType.DMA((16,))]
    v = v.reshape(96, 2, 16, 128)
    return call(z_back_kernel, (C, 8, 16, NZ), v, linear_0, linear_1, table, outs=ANY, scratch=scratch)


def solution(mesh):
    shape = (4, 8, 4, 2, 2)
    fine = Mesh(mesh.devices.reshape(shape), GX + GY)
    spec = P(None, GX, GY, None)
    return jax.shard_map(
        on_device,
        mesh=fine,
        in_specs=(spec, spec, P(), P()),
        out_specs=spec,
        check_vma=False,
    )
```
